32 devices in a mesh: sta: 16 (over z, y, x), win: 2 (over core).
Axes of the slice: x: 2, y: 2, z: 4, core: 2. Of those that a mesh axis runs over, the one named last changes fastest.
Arguments:
- spectra: float32 [4, 64, 2, 3, 1664], P('win', 'sta')
- flags: int32 [4, 64], P('win', 'sta'), may hold values 0 or 1
- owners: int32 [4], replicated, may hold values from 0 to 15, as said below
- source_slots: int32 [4, 4], replicated, may hold values from 0 to 3, as said below
Outputs:
- correlations: float32 [4, 4, 3, 64, 3, 768], P(None, None, None, 'sta')
The draws below stay inside these ranges and needn't reach their ends.
Inputs may be any that keep to these rules, and one draw needn't show every extreme that they name: `owners`: the index of a block of 4 stations along sta. `source_slots`: distinct within a step.
All inputs are finite; a program needn't handle non-finite values. No bound on the sum of `flags` on one device may be relied on, other than what follows from the above.
Results may differ from the reference program's by a relative error of at most 0.0037.
Values sent between devices are 32-bit elements; how exact they have to be, the bound alone decides.
No kernel may reach another device: no remote copies, remote signals or barrier semaphores. Data moves between devices by JAX's collectives and lax.ppermute only.
A program may use at most 64 MiB of HBM per device.

```python
import math
import jax
import jax.numpy as jnp
from jax import lax

NF = 1664
NLAG = 768
SRC = 4
STEPS = 4
WIN_DEV = 2
REC_DEV = 4
STATIONS = 64
WINDOWS = 4
N_WIN = 2


def draw_spectra(key, part):
    first, second, third = jax.random.split(key, 3)
    shape = (WINDOWS, STATIONS, 2, 3, NF)
    station_scale = jnp.exp(jax.random.uniform(first, (1, STATIONS, 1, 1, 1), jnp.float32, 0.0, math.log(10.0)))
    bin_scale = jnp.exp(jax.random.uniform(second, (WINDOWS, STATIONS, 1, 3, NF), jnp.float32, -1.2, 1.2))
    base = jax.random.normal(third, shape, jnp.float32)
    return base * bin_scale * station_scale


def draw_owners(key, part):
    blocks = STATIONS // REC_DEV
    first, second = jax.random.split(jax.random.fold_in(key, 11))
    picks = jax.random.randint(first, (STEPS,), 0, blocks)
    order = jax.random.permutation(second, STEPS)
    picks = picks.at[order[0]].set(blocks - 1)
    return picks.at[order[1]].set(0).astype(jnp.int32)


def draw_source_slots(key, part):
    rows = []
    for step in range(STEPS):
        step_key = jax.random.fold_in(key, 100 + step)
        first, second = jax.random.split(step_key)
        perm = jax.random.permutation(first, REC_DEV).astype(jnp.int32)
        target = REC_DEV - 1 if step % 2 == 0 else 0
        head = perm[:SRC]
        present = jnp.any(head == target)
        position = jax.random.randint(second, (), 0, SRC)
        replaced = head.at[position].set(target)
        rows.append(jnp.where(present, head, replaced))
    return jnp.stack(rows).astype(jnp.int32)


def place_ends(drawn, stream_key, low, largest):
    longest = drawn.shape.index(max(drawn.shape))
    spots = []
    for shift in (0, 1):
        where = [jax.random.randint(jax.random.fold_in(stream_key, axis), (), 0, length) for axis, length in enumerate(drawn.shape)]
        where[longest] = (where[longest] + shift) % drawn.shape[longest]
        spots.append(tuple(where))
    return drawn.at[spots[0]].set(low).at[spots[1]].set(largest)


def setup_inputs(seed: int = 0) -> dict:
    key_of = jax.random.split(jax.random.key(seed), 5)
    spectra = draw_spectra(jax.random.fold_in(key_of[4], 71), 0)
    flags = place_ends((jax.random.randint(key_of[1], (WINDOWS, STATIONS), 0, 4) < 3).astype(jnp.int32), jax.random.fold_in(key_of[1], 1), 0, 1)
    owners = draw_owners(jax.random.fold_in(key_of[4], 71), 0)
    source_slots = draw_source_slots(jax.random.fold_in(key_of[4], 71), 0)
    return {"spectra": spectra, "flags": flags, "owners": owners, "source_slots": source_slots}


def whiten(spectra):
    shape = spectra.shape
    blocks = spectra.reshape(shape[0], shape[1], 2, 3, shape[4] // 64, 64)
    power = lax.optimization_barrier(jnp.mean(blocks * blocks, axis=(2, 3, 5), keepdims=True))
    return (blocks / jnp.sqrt(power + 1e-06)).reshape(shape)

def lag_table(bins, lags, windows):
    freq = jnp.arange(bins, dtype=jnp.int32) + 360
    shift = jnp.arange(lags, dtype=jnp.int32) - lags // 2
    phase = jnp.mod(freq[:, None] * shift[None, :], 7200).astype(jnp.float32) * (2.0 * math.pi / 7200.0)
    scale = 1.0 / math.sqrt(windows * bins)
    return jnp.concatenate([jnp.cos(phase) * scale, -jnp.sin(phase) * scale], axis=0).astype(jnp.bfloat16)

def correlate(picked, receivers, table):
    src_re = picked[:, :, 0][:, :, :, None, None, :]
    src_im = picked[:, :, 1][:, :, :, None, None, :]
    rec_re = receivers[:, :, 0][:, None, None, :, :, :]
    rec_im = receivers[:, :, 1][:, None, None, :, :, :]
    real = lax.optimization_barrier(jnp.sum(src_re * rec_re + src_im * rec_im, axis=0))
    imag = lax.optimization_barrier(jnp.sum(src_im * rec_re - src_re * rec_im, axis=0))
    shape = real.shape
    bins = shape[4]
    rows = jnp.concatenate([real.reshape(-1, bins), imag.reshape(-1, bins)], axis=1).astype(jnp.bfloat16)
    lagged = jnp.dot(rows, table, preferred_element_type=jnp.float32)
    return lagged.reshape(shape[0], shape[1], shape[2], shape[3], table.shape[1])

def reference(spectra, flags, owners, source_slots):
    whitened = whiten(spectra)
    weighted = whitened * flags.astype(jnp.float32)[:, :, None, None, None]
    table = lag_table(NF, NLAG, WINDOWS)
    results = []
    for step in range(STEPS):
        stations = (owners[step] * REC_DEV + source_slots[step]).astype(jnp.int32)
        picked = jnp.take(weighted, stations, axis=1)
        total = jnp.zeros((SRC, 3, STATIONS, 3, NLAG), jnp.float32)
        for group in range(N_WIN):
            low = group * WIN_DEV
            total = total + correlate(picked[low:low + WIN_DEV], weighted[low:low + WIN_DEV], table)
        results.append(total)
    return jnp.stack(results)
```

```python
import functools
import math

import jax
import jax.numpy as jnp
import numpy as np
from jax import lax
from jax.experimental import pallas as pl
from jax.experimental.pallas import tpu as pltpu
from jax.sharding import PartitionSpec as P

NLAG = 768
LANES = 128
VMEM = 40 * 1024 * 1024


def lag_table(bins, lags, windows):
    freq = np.arange(bins, dtype=np.int64) + 360
    shift = np.arange(lags, dtype=np.int64) - lags // 2
    phase = np.mod(freq[:, None] * shift[None, :], 7200).astype(np.float32) * np.float32(
        2.0 * math.pi / 7200.0
    )
    scale = np.float32(1.0 / math.sqrt(windows * bins))
    real = (np.cos(phase) * scale).reshape(bins // LANES, 1, LANES, lags)
    imag = (-np.sin(phase) * scale).reshape(bins // LANES, 1, LANES, lags)
    return np.concatenate([real, imag], axis=1).reshape(2 * bins, lags).astype(jnp.bfloat16)


def whiten_kernel(flags, x_ref, pieces_ref, rec_ref):
    wins, stas, comps, _, bins = x_ref.shape
    tiles = bins // LANES
    lane = lax.broadcasted_iota(jnp.int32, (wins * stas, LANES), 1)
    left = lane < 64
    sums = []
    for w in range(wins):
        for s in range(stas):
            x = x_ref[w, s]
            sums.append(jnp.sum(jnp.sum(x * x, axis=0), axis=0, keepdims=True))
    power = jnp.concatenate(sums, axis=0)
    weight = jnp.concatenate(
        [
            jnp.full((1, LANES), flags[w, s].astype(jnp.float32), jnp.float32)
            for w in range(wins)
            for s in range(stas)
        ],
        axis=0,
    )
    scales = []
    for c in range(tiles):
        tile = power[:, c * LANES : (c + 1) * LANES]
        low = jnp.sum(jnp.where(left, tile, 0.0), axis=1, keepdims=True)
        high = jnp.sum(jnp.where(left, 0.0, tile), axis=1, keepdims=True)
        mean = jnp.where(left, low, high) * (1.0 / (64 * 2 * comps))
        scales.append(weight / jnp.sqrt(mean + 1e-06))
    scale = jnp.concatenate(scales, axis=1)
    for w in range(wins):
        for s in range(stas):
            k = w * stas + s
            row = scale[k : k + 1]
            for i in range(comps):
                y = x_ref[w, s, i] * row
                for part in range(2):
                    rec_ref[w, part, pl.ds(i * stas + s, 1), :] = y[part : part + 1]
                    for c in range(tiles):
                        pieces_ref[(s * wins + w) * 2 + part, pl.ds(i * tiles + c, 1), :] = y[
                            part : part + 1, c * LANES : (c + 1) * LANES
                        ]
    rest = pieces_ref.shape[1] - comps * tiles
    if rest:
        for k in range(wins * stas * 2):
            pieces_ref[k, pl.ds(comps * tiles, rest), :] = jnp.zeros((rest, LANES), jnp.float32)
    spare = rec_ref.shape[2] - comps * stas
    if spare:
        for w in range(wins):
            for part in range(2):
                rec_ref[w, part, pl.ds(comps * stas, spare), :] = jnp.zeros(
                    (spare, bins), jnp.float32
                )


def whiten(spectra, flags):
    wins, stas, _, comps, bins = spectra.shape
    rows = -(-comps * (bins // LANES) // 8) * 8
    recs = -(-comps * stas // 8) * 8
    return pl.pallas_call(
        whiten_kernel,
        out_shape=(
            jax.ShapeDtypeStruct((wins * stas * 2, rows, LANES), jnp.float32),
            jax.ShapeDtypeStruct((wins, 2, recs, bins), jnp.float32),
        ),
        in_specs=[
            pl.BlockSpec(memory_space=pltpu.SMEM),
            pl.BlockSpec(memory_space=pltpu.VMEM),
        ],
        out_specs=(
            pl.BlockSpec(memory_space=pltpu.VMEM),
            pl.BlockSpec(memory_space=pltpu.VMEM),
        ),
        compiler_params=pltpu.CompilerParams(vmem_limit_bytes=VMEM),
        name="whiten",
    )(flags, jnp.transpose(spectra, (0, 1, 3, 2, 4)))


def pick_kernel(owners, core, got_ref, keep_ref, send_ref):
    for t in range(keep_ref.shape[0]):
        keep_ref[t] = got_ref[owners[2 * t + core[0]]]
        send_ref[t] = got_ref[owners[2 * t + 1 - core[0]]]


def pick(owners, core, got):
    steps = owners.shape[0]
    shape = jax.ShapeDtypeStruct((steps // 2,) + got.shape[1:], jnp.float32)
    smem = pl.BlockSpec(memory_space=pltpu.SMEM)
    vmem = pl.BlockSpec(memory_space=pltpu.VMEM)
    return pl.pallas_call(
        pick_kernel,
        out_shape=(shape, shape),
        in_specs=[smem, smem, vmem],
        out_specs=(vmem, vmem),
        name="pick",
    )(owners, core, got)


def correlate_kernel(
    slots, where, s0, s1, s2, s3, r0, r1, table_hbm, out_ref, src, rec, table, lhs, sems, tsem
):
    _, _, groups, steps, _, _ = src.shape
    wins = groups
    bins = r0.shape[3]
    tiles = bins // LANES
    place, z, core = where[0], where[1], where[2]
    spots = (place, place ^ (1 + core), place ^ (2 - core), place ^ 3)
    copies = [
        pltpu.make_async_copy(ref, src.at[spot], sems.at[n])
        for n, (ref, spot) in enumerate(zip((s0, s1, s2, s3), spots))
    ]
    table_copy = pltpu.make_async_copy(table_hbm, table, tsem)
    for copy in copies:
        copy.start()
    table_copy.start()
    for g, ref in enumerate((r0, r1)):
        for w in range(wins):
            for part in range(2):
                both = ref[w, part, 0:12, :]
                rec[g, w, part, 0:12, :] = both
                rec[g, w, part, 12:24, :] = both
    for copy in copies:
        copy.wait()
    upper = lax.broadcasted_iota(jnp.int32, (8, LANES), 0) < 4

    def chunk(c, carry):
        lanes = pl.ds(pl.multiple_of(c * LANES, LANES), LANES)
        receivers = [
            [[rec[g, w, part, :, lanes] for part in range(2)] for w in range(wins)]
            for g in range(groups)
        ]
        for block in range(steps * 12 // 4):
            real_tiles, imag_tiles = [], []
            for pair in range(2):
                numbers = (block * 4 + pair * 2, block * 4 + pair * 2 + 1)
                real = [None] * 3
                imag = [None] * 3
                for g in range(groups):
                    for w in range(wins):
                        spread = []
                        for part in range(2):
                            rows = []
                            for n in numbers:
                                t, s, i = n // 12, (n // 3) % 4, n % 3
                                line = src[
                                    w * 2 + part,
                                    slots[t, s] ^ z,
                                    g,
                                    t,
                                    pl.ds(i * tiles + c, 1),
                                    :,
                                ]
                                rows.append(jnp.broadcast_to(line, (8, LANES)))
                            spread.append((rows[0], jnp.where(upper, rows[0], rows[1]), rows[1]))
                        for k in range(3):
                            rr = receivers[g][w][0][8 * k : 8 * k + 8]
                            ri = receivers[g][w][1][8 * k : 8 * k + 8]
                            sr, si = spread[0][k], spread[1][k]
                            re = sr * rr + si * ri
                            im = si * rr - sr * ri
                            real[k] = re if real[k] is None else real[k] + re
                            imag[k] = im if imag[k] is None else imag[k] + im
                real_tiles += real
                imag_tiles += imag
            at = pl.ds(block * 48, 48)
            base = c * 2 * LANES
            lhs[at, pl.ds(pl.multiple_of(base, LANES), LANES)] = jnp.concatenate(
                real_tiles, axis=0
            ).astype(jnp.bfloat16)
            lhs[at, pl.ds(pl.multiple_of(base + LANES, LANES), LANES)] = jnp.concatenate(
                imag_tiles, axis=0
            ).astype(jnp.bfloat16)
        return carry

    lax.fori_loop(0, tiles, chunk, 0)
    table_copy.wait()
    for n in range(out_ref.shape[2] // 256):
        lags = pl.ds(n * 256, 256)
        result = jnp.dot(lhs[...], table[:, lags], preferred_element_type=jnp.float32)
        for k in range(out_ref.shape[0]):
            out_ref[k, :, lags] = result[4 * k : 4 * k + 4]


def correlate(slots, where, sources, own, other, table):
    steps = sources[0].shape[2]
    bins = own.shape[3]
    rows = steps * 4 * 3 * 12
    lags = table.shape[1]
    vmem = pl.BlockSpec(memory_space=pltpu.VMEM)
    smem = pl.BlockSpec(memory_space=pltpu.SMEM)
    hbm = pl.BlockSpec(memory_space=pltpu.HBM)
    return pl.pallas_call(
        correlate_kernel,
        out_shape=jax.ShapeDtypeStruct((rows // 4, 4, lags), jnp.float32),
        in_specs=[smem, smem] + [vmem] * 6 + [hbm],
        out_specs=vmem,
        scratch_shapes=[
            pltpu.VMEM((4,) + sources[0].shape, jnp.float32),
            pltpu.VMEM((2, 2, 2, 24, bins), jnp.float32),
            pltpu.VMEM(table.shape, jnp.bfloat16),
            pltpu.VMEM((rows, 2 * bins), jnp.bfloat16),
            pltpu.SemaphoreType.DMA((4,)),
            pltpu.SemaphoreType.DMA,
        ],
        compiler_params=pltpu.CompilerParams(vmem_limit_bytes=VMEM),
        name="correlate",
    )(slots, where, *sources, own, other, table)


def join_kernel(core, own, other, out, sems):
    half = own.shape[0]
    copies = []
    for t in range(half):
        copies.append(pltpu.make_async_copy(own.at[t], out.at[2 * t + core[0]], sems.at[2 * t]))
        copies.append(
            pltpu.make_async_copy(other.at[t], out.at[2 * t + 1 - core[0]], sems.at[2 * t + 1])
        )
    for copy in copies:
        copy.start()
    for copy in copies:
        copy.wait()


def join(core, own, other):
    vmem = pl.BlockSpec(memory_space=pltpu.VMEM)
    return pl.pallas_call(
        join_kernel,
        out_shape=jax.ShapeDtypeStruct((2 * own.shape[0],) + own.shape[1:], jnp.float32),
        in_specs=[pl.BlockSpec(memory_space=pltpu.SMEM), vmem, vmem],
        out_specs=pl.BlockSpec(memory_space=pltpu.HBM),
        scratch_shapes=[pltpu.SemaphoreType.DMA((2 * own.shape[0],))],
        name="join",
    )(core, own, other)


def swap(value):
    return lax.ppermute(value, "win", [(0, 1), (1, 0)])


def on_device(spectra, flags, owners, source_slots):
    wins, stas, _, comps, bins = spectra.shape
    steps, sources = source_slots.shape
    place = lax.axis_index("sta") % 4
    z = lax.axis_index("sta") // 4
    core = lax.axis_index("win")
    core_arg = core.astype(jnp.int32)[None]
    blocks = lax.axis_size("sta")
    pieces, own = whiten(spectra, flags)
    other = swap(own)
    got = lax.all_to_all(pieces, "sta", 0, 0)
    keep, send = pick(owners, core_arg, got)
    mine = jnp.stack([keep, swap(send)])

    def partner(bits):
        return [(i, i ^ bits) for i in range(blocks)]

    def by_core(first, second):
        bits = (first, second)
        return [(2 * i + c, 2 * (i ^ bits[c]) + c) for i in range(blocks) for c in range(2)]

    column = jnp.stack([mine] + [lax.ppermute(mine, "sta", partner(4 * k)) for k in (1, 2, 3)])
    near = lax.ppermute(column, ("sta", "win"), by_core(1, 2))
    next_ = lax.ppermute(column, ("sta", "win"), by_core(2, 1))
    far = lax.ppermute(near, ("sta", "win"), by_core(2, 1))
    slots = lax.dynamic_slice(
        source_slots.reshape(steps // 2, 2, sources), (0, core, 0), (steps // 2, 1, sources)
    )[:, 0]
    where = jnp.stack([place, z, core]).astype(jnp.int32)
    table = jnp.asarray(lag_table(bins, NLAG, wins * lax.axis_size("win")))
    half = correlate(slots, where, (column, near, next_, far), own, other, table)
    half = half.reshape(steps // 2, -1, 4, NLAG)
    whole = join(core_arg, half, swap(half))
    return whole.reshape(steps, sources, comps, comps, stas, NLAG).transpose(0, 1, 2, 4, 3, 5)


def spread(value, axis, source):
    kept = jnp.where(lax.axis_index(axis) == source, value, 0).astype(value.dtype)
    return lax.psum(kept, axis)


def cross(picked, receivers, table):
    src_re = picked[:, :, 0][:, :, :, None, None, :]
    src_im = picked[:, :, 1][:, :, :, None, None, :]
    rec_re = receivers[:, :, 0][:, None, None, :, :, :]
    rec_im = receivers[:, :, 1][:, None, None, :, :, :]
    real = jnp.sum(src_re * rec_re + src_im * rec_im, axis=0)
    imag = jnp.sum(src_im * rec_re - src_re * rec_im, axis=0)
    shape = real.shape
    both = jnp.stack(
        [part.reshape(shape[:4] + (shape[4] // LANES, LANES)) for part in (real, imag)], axis=5
    )
    rows = both.reshape(-1, 2 * shape[4]).astype(jnp.bfloat16)
    lagged = jnp.dot(rows, table, preferred_element_type=jnp.float32)
    return lagged.reshape(shape[:4] + (table.shape[1],))


def on_device_general(spectra, flags, owners, source_slots):
    shape = spectra.shape
    blocks = spectra.reshape(shape[:4] + (shape[4] // 64, 64))
    power = jnp.mean(blocks * blocks, axis=(2, 3, 5), keepdims=True)
    whitened = (blocks / jnp.sqrt(power + 1e-06)).reshape(shape)
    weighted = whitened * flags.astype(jnp.float32)[:, :, None, None, None]
    table = jnp.asarray(lag_table(shape[4], NLAG, shape[0] * lax.axis_size("win")))
    outputs = []
    for step in range(source_slots.shape[0]):
        chosen = jnp.take(weighted, source_slots[step], axis=1)
        picked = spread(chosen, "sta", owners[step])
        outputs.append(lax.psum(cross(picked, weighted, table), "win"))
    return jnp.stack(outputs)


def solution(mesh):
    small = mesh.shape["sta"] == 16 and mesh.shape["win"] == 2
    return jax.shard_map(
        on_device if small else on_device_general,
        mesh=mesh,
        in_specs=(P("win", "sta", None, None, None), P("win", "sta"), P(), P()),
        out_specs=P(None, None, None, "sta", None, None),
        check_vma=False,
    )
```

```python
import functools
import math

import jax
import jax.numpy as jnp
import numpy as np
from jax import lax
from jax.experimental import pallas as pl
from jax.experimental.pallas import tpu as pltpu
from jax.sharding import PartitionSpec as P

NLAG = 768
LANES = 128
MIB = 1024 * 1024


def lag_table(bins, lags, windows):
    freq = np.arange(bins, dtype=np.int64) + 360
    shift = np.arange(lags, dtype=np.int64) - lags // 2
    phase = np.mod(freq[:, None] * shift[None, :], 7200).astype(np.float32) * np.float32(
        2.0 * math.pi / 7200.0
    )
    scale = np.float32(1.0 / math.sqrt(windows * bins))
    real = (np.cos(phase) * scale).reshape(bins // LANES, 1, LANES, lags)
    imag = (-np.sin(phase) * scale).reshape(bins // LANES, 1, LANES, lags)
    return np.concatenate([real, imag], axis=1).reshape(2 * bins, lags).astype(jnp.bfloat16)


def whiten_kernel(flags_hbm, x_hbm, pieces_ref, rec_ref, flags, x_ref, sems):
    copies = (
        pltpu.make_async_copy(flags_hbm, flags, sems.at[0]),
        pltpu.make_async_copy(x_hbm, x_ref, sems.at[1]),
    )
    for copy in copies:
        copy.start()
    for copy in copies:
        copy.wait()
    wins, stas, comps, _, bins = x_ref.shape
    core = lax.axis_index("win")
    place = ((0, 1 + core), (2 - core, 3))
    tiles = bins // LANES
    lane = lax.broadcasted_iota(jnp.int32, (wins * stas, LANES), 1)
    left = lane < 64
    sums = []
    for w in range(wins):
        for s in range(stas):
            x = x_ref[w, s]
            sums.append(jnp.sum(jnp.sum(x * x, axis=0), axis=0, keepdims=True))
    power = jnp.concatenate(sums, axis=0)
    weight = jnp.concatenate(
        [
            jnp.full((1, LANES), flags[w, s].astype(jnp.float32), jnp.float32)
            for w in range(wins)
            for s in range(stas)
        ],
        axis=0,
    )
    scales = []
    for c in range(tiles):
        tile = power[:, c * LANES : (c + 1) * LANES]
        low = jnp.sum(jnp.where(left, tile, 0.0), axis=1, keepdims=True)
        high = jnp.sum(jnp.where(left, 0.0, tile), axis=1, keepdims=True)
        mean = jnp.where(left, low, high) * (1.0 / (64 * 2 * comps))
        scales.append(weight / jnp.sqrt(mean + 1e-06))
    scale = jnp.concatenate(scales, axis=1)
    for w in range(wins):
        for s in range(stas):
            k = w * stas + s
            row = scale[k : k + 1]
            for i in range(comps):
                y = x_ref[w, s, i] * row
                for part in range(2):
                    rec_ref[w, part, pl.ds(i * stas + s, 1), :] = y[part : part + 1]
                    for c in range(tiles):
                        pieces_ref[4 * s + place[w][part], pl.ds(i * tiles + c, 1), :] = y[
                            part : part + 1, c * LANES : (c + 1) * LANES
                        ]
    rest = pieces_ref.shape[1] - comps * tiles
    if rest:
        for k in range(wins * stas * 2):
            pieces_ref[k, pl.ds(comps * tiles, rest), :] = jnp.zeros((rest, LANES), jnp.float32)
    spare = rec_ref.shape[2] - comps * stas
    if spare:
        for w in range(wins):
            for part in range(2):
                rec_ref[w, part, pl.ds(comps * stas, spare), :] = jnp.zeros(
                    (spare, bins), jnp.float32
                )


def whiten(spectra, flags):
    wins, stas, _, comps, bins = spectra.shape
    rows = -(-comps * (bins // LANES) // 8) * 8
    recs = -(-comps * stas // 8) * 8
    return pl.pallas_call(
        whiten_kernel,
        out_shape=(
            jax.ShapeDtypeStruct((wins * stas * 2, rows, LANES), jnp.float32),
            jax.ShapeDtypeStruct((wins, 2, recs, bins), jnp.float32),
        ),
        in_specs=[pl.BlockSpec(memory_space=pltpu.HBM)] * 2,
        out_specs=(
            pl.BlockSpec(memory_space=pltpu.VMEM),
            pl.BlockSpec(memory_space=pltpu.VMEM),
        ),
        scratch_shapes=[
            pltpu.SMEM(flags.shape, jnp.int32),
            pltpu.VMEM((wins, stas, comps, 2, bins), jnp.float32),
            pltpu.SemaphoreType.DMA((2,)),
        ],
        compiler_params=pltpu.CompilerParams(vmem_limit_bytes=61 * MIB),
        name="whiten",
    )(flags, jnp.transpose(spectra, (0, 1, 3, 2, 4)))


def pick_kernel(params, got_ref, before, keep_ref, send_ref):
    half = keep_ref.shape[0]
    for t in range(half):
        keep_ref[t] = got_ref[params[3 + t]]
        send_ref[t] = got_ref[params[3 + half + t]]


def pick(params, got, before, steps):
    shape = jax.ShapeDtypeStruct((steps // 2,) + got.shape[1:], jnp.float32)
    smem = pl.BlockSpec(memory_space=pltpu.SMEM)
    vmem = pl.BlockSpec(memory_space=pltpu.VMEM)
    return pl.pallas_call(
        pick_kernel,
        out_shape=(shape, shape),
        in_specs=[smem, vmem, vmem],
        out_specs=(vmem, vmem),
        compiler_params=pltpu.CompilerParams(vmem_limit_bytes=8 * MIB),
        name="pick",
    )(params, got, before)


def pack_kernel(*refs, count):
    for n in range(count):
        refs[-1][n] = refs[n][...]


def pack(values, before):
    vmem = pl.BlockSpec(memory_space=pltpu.VMEM)
    return pl.pallas_call(
        functools.partial(pack_kernel, count=len(values)),
        out_shape=jax.ShapeDtypeStruct((len(values),) + values[0].shape, values[0].dtype),
        in_specs=[vmem] * (len(values) + len(before)),
        out_specs=vmem,
        compiler_params=pltpu.CompilerParams(vmem_limit_bytes=8 * MIB),
        name="pack",
    )(*values, *before)


def load_kernel(table_hbm, after, out_ref, sem):
    copy = pltpu.make_async_copy(table_hbm, out_ref, sem)
    copy.start()
    copy.wait()


def load(table, after):
    vmem = pl.BlockSpec(memory_space=pltpu.VMEM)
    return pl.pallas_call(
        load_kernel,
        out_shape=jax.ShapeDtypeStruct(table.shape, table.dtype),
        in_specs=[pl.BlockSpec(memory_space=pltpu.HBM), vmem],
        out_specs=vmem,
        scratch_shapes=[pltpu.SemaphoreType.DMA],
        compiler_params=pltpu.CompilerParams(vmem_limit_bytes=8 * MIB),
        cost_estimate=pl.CostEstimate(flops=0, bytes_accessed=5 * MIB, transcendentals=0),
        name="load",
    )(table, after)


def correlate_kernel(params, *refs):
    firsts, rests = refs[0:8:2], refs[1:8:2]
    receivers_in, table, out_ref, rec, lhs = refs[8:10], refs[10], refs[11], refs[12], refs[13]
    groups, steps, _, _ = firsts[0].shape
    depth = 1 + rests[0].shape[0]
    tiles = rec.shape[4] // LANES
    window, part = params[1], params[2]
    kinds = ((window, part), (part, window))
    signs = []
    for g, (w, p) in enumerate(kinds):
        signs.append(1.0 - 2.0 * p.astype(jnp.float32))
        for other_w in range(2):
            for other_p in range(2):
                rows = receivers_in[g][w ^ other_w, p ^ other_p, 0:12, :]
                rec[g, other_w, other_p, 0:12, :] = rows
                rec[g, other_w, other_p, 12:24, :] = rows
    spots = (((0, 1), (2, 3)), ((0, 2), (1, 3)))
    upper = lax.broadcasted_iota(jnp.int32, (8, LANES), 0) < 4

    def source(spot, g, n, c):
        t, offset, i = n // (3 * depth), (n // 3) % depth, n % 3
        row = pl.ds(i * tiles + c, 1)
        if offset:
            line = rests[spot][offset - 1, g, t, row, :]
        else:
            line = firsts[spot][g, t, row, :]
        return jnp.broadcast_to(line, (8, LANES))

    def chunk(c, carry):
        lanes = pl.ds(pl.multiple_of(c * LANES, LANES), LANES)
        receivers = [
            [[rec[g, w, p, :, lanes] for p in range(2)] for w in range(2)] for g in range(groups)
        ]
        for block in range(steps * depth * 3 // 4):
            real_tiles, imag_tiles = [], []
            for pair in range(2):
                numbers = (block * 4 + pair * 2, block * 4 + pair * 2 + 1)
                real = [0.0] * 3
                imag = [0.0] * 3
                for g in range(groups):
                    part_imag = [0.0] * 3
                    for w in range(2):
                        spread = []
                        for p in range(2):
                            rows = [source(spots[g][w][p], g, n, c) for n in numbers]
                            spread.append((rows[0], jnp.where(upper, rows[0], rows[1]), rows[1]))
                        for k in range(3):
                            ra = receivers[g][w][0][8 * k : 8 * k + 8]
                            rb = receivers[g][w][1][8 * k : 8 * k + 8]
                            a, b = spread[0][k], spread[1][k]
                            real[k] += a * ra + b * rb
                            part_imag[k] += b * ra - a * rb
                    for k in range(3):
                        imag[k] += signs[g] * part_imag[k]
                real_tiles += real
                imag_tiles += imag
            at = pl.ds(block * 48, 48)
            base = c * 2 * LANES
            lhs[at, pl.ds(pl.multiple_of(base, LANES), LANES)] = jnp.concatenate(
                real_tiles, axis=0
            ).astype(jnp.bfloat16)
            lhs[at, pl.ds(pl.multiple_of(base + LANES, LANES), LANES)] = jnp.concatenate(
                imag_tiles, axis=0
            ).astype(jnp.bfloat16)
        return carry

    lax.fori_loop(0, tiles, chunk, 0)
    for n in range(out_ref.shape[3] // 256):
        lags = pl.ds(n * 256, 256)
        result = jnp.dot(lhs[...], table[:, lags], preferred_element_type=jnp.float32)
        for t in range(steps):
            for offset in range(depth):
                first = params[3 + 2 * steps + depth * t + offset] * 9
                for k in range(9):
                    row = 4 * ((t * depth + offset) * 9 + k)
                    out_ref[t, first + k, :, lags] = result[row : row + 4]


def correlate(params, sources, own, other, table):
    steps = sources[0].shape[1]
    depth = 1 + sources[1].shape[0]
    bins = own.shape[3]
    lags = table.shape[1]
    vmem = pl.BlockSpec(memory_space=pltpu.VMEM)
    return pl.pallas_call(
        correlate_kernel,
        out_shape=jax.ShapeDtypeStruct((steps, depth * 9, 4, lags), jnp.float32),
        in_specs=[pl.BlockSpec(memory_space=pltpu.SMEM)] + [vmem] * 11,
        out_specs=vmem,
        scratch_shapes=[
            pltpu.VMEM((2, 2, 2, 24, bins), jnp.float32),
            pltpu.VMEM((steps * depth * 3 * 12, 2 * bins), jnp.bfloat16),
        ],
        compiler_params=pltpu.CompilerParams(vmem_limit_bytes=20 * MIB),
        name="correlate",
    )(params, *sources, own, other, table)


def write_steps(half, out, core, sems):
    parts = sems.shape[1]
    size = half.shape[1] // parts
    copies = [
        pltpu.make_async_copy(
            half.at[t, pl.ds(n * size, size)],
            out.at[2 * t + core, pl.ds(n * size, size)],
            sems.at[t, n],
        )
        for t in range(half.shape[0])
        for n in range(parts)
    ]
    for copy in copies:
        copy.start()
    for copy in copies:
        copy.wait()


def put_kernel(own, out, sems):
    write_steps(own, out, lax.axis_index("win"), sems)


def put(own):
    return pl.pallas_call(
        put_kernel,
        out_shape=jax.ShapeDtypeStruct((2 * own.shape[0],) + own.shape[1:], own.dtype),
        in_specs=[pl.BlockSpec(memory_space=pltpu.VMEM)],
        out_specs=pl.BlockSpec(memory_space=pltpu.HBM),
        scratch_shapes=[pltpu.SemaphoreType.DMA((own.shape[0], 4))],
        compiler_params=pltpu.CompilerParams(vmem_limit_bytes=8 * MIB),
        name="put",
    )(own)


def join_kernel(other, whole, out, sems):
    write_steps(other, out, 1 - lax.axis_index("win"), sems)


def join(other, whole):
    hbm = pl.BlockSpec(memory_space=pltpu.HBM)
    return pl.pallas_call(
        join_kernel,
        out_shape=jax.ShapeDtypeStruct(whole.shape, whole.dtype),
        in_specs=[pl.BlockSpec(memory_space=pltpu.VMEM), hbm],
        out_specs=hbm,
        scratch_shapes=[pltpu.SemaphoreType.DMA((other.shape[0], 4))],
        input_output_aliases={1: 0},
        compiler_params=pltpu.CompilerParams(vmem_limit_bytes=8 * MIB),
        name="join",
    )(other, whole)


def swap(value):
    return lax.ppermute(value, "win", [(0, 1), (1, 0)])


def on_device(spectra, flags, owners, source_slots):
    wins, stas, _, comps, bins = spectra.shape
    steps, sources = source_slots.shape
    at = lax.axis_index("sta")
    core = lax.axis_index("win")
    blocks = lax.axis_size("sta")
    pairs = owners.reshape(steps // 2, 2)
    slots = source_slots.reshape(steps // 2, 2, sources)
    z, place = at >> 2, at & 3
    high, low = place >> 1, place & 1
    mine = jnp.where(core == 0, slots[:, 0], slots[:, 1])
    held = z ^ jnp.arange(sources, dtype=jnp.int32)
    order = jnp.arange(sources, dtype=jnp.int32)
    found = jnp.sum(
        jnp.where(mine[:, None, :] == held[None, :, None], order[None, None, :], 0), axis=2
    )
    params = jnp.concatenate(
        [
            jnp.stack([core, jnp.where(core == 0, high, low), jnp.where(core == 0, low, high)]),
            jnp.where(core == 0, pairs[:, 0], pairs[:, 1]),
            jnp.where(core == 0, pairs[:, 1], pairs[:, 0]),
            found.reshape(-1),
        ]
    ).astype(jnp.int32)
    pieces, own = whiten(spectra, flags)
    other = swap(own)
    got = lax.all_to_all(pieces, "sta", 0, 0)
    keep, send = pick(params, got, other, steps)
    mine = jnp.stack([keep, swap(send)])

    def partner(bits):
        return [(i, i ^ bits) for i in range(blocks)]

    def by_core(first, second):
        bits = (first, second)
        return [(2 * i + c, 2 * (i ^ bits[c]) + c) for i in range(blocks) for c in range(2)]

    def plane(value):
        near = lax.ppermute(value, ("sta", "win"), by_core(1, 2))
        side = lax.ppermute(value, ("sta", "win"), by_core(2, 1))
        return value, near, side, lax.ppermute(value, "sta", partner(3))

    column = [lax.ppermute(mine, "sta", partner(4 * k)) for k in (1, 2, 3)]
    first = plane(mine)
    rest = plane(pack(column, first[1:]))
    sources_in = [value for spot in zip(first, rest) for value in spot]
    table = jnp.asarray(lag_table(bins, NLAG, wins * lax.axis_size("win")))
    table = load(table, mine)
    half = correlate(params, sources_in, own, other, table)
    whole = join(swap(half), put(half))
    return whole.reshape(steps, sources, comps, comps, stas, NLAG).transpose(0, 1, 2, 4, 3, 5)


def spread(value, axis, source):
    kept = jnp.where(lax.axis_index(axis) == source, value, 0).astype(value.dtype)
    return lax.psum(kept, axis)


def cross(picked, receivers, table):
    src_re = picked[:, :, 0][:, :, :, None, None, :]
    src_im = picked[:, :, 1][:, :, :, None, None, :]
    rec_re = receivers[:, :, 0][:, None, None, :, :, :]
    rec_im = receivers[:, :, 1][:, None, None, :, :, :]
    real = jnp.sum(src_re * rec_re + src_im * rec_im, axis=0)
    imag = jnp.sum(src_im * rec_re - src_re * rec_im, axis=0)
    shape = real.shape
    both = jnp.stack(
        [part.reshape(shape[:4] + (shape[4] // LANES, LANES)) for part in (real, imag)], axis=5
    )
    rows = both.reshape(-1, 2 * shape[4]).astype(jnp.bfloat16)
    lagged = jnp.dot(rows, table, preferred_element_type=jnp.float32)
    return lagged.reshape(shape[:4] + (table.shape[1],))


def on_device_general(spectra, flags, owners, source_slots):
    shape = spectra.shape
    blocks = spectra.reshape(shape[:4] + (shape[4] // 64, 64))
    power = jnp.mean(blocks * blocks, axis=(2, 3, 5), keepdims=True)
    whitened = (blocks / jnp.sqrt(power + 1e-06)).reshape(shape)
    weighted = whitened * flags.astype(jnp.float32)[:, :, None, None, None]
    table = jnp.asarray(lag_table(shape[4], NLAG, shape[0] * lax.axis_size("win")))
    outputs = []
    for step in range(source_slots.shape[0]):
        chosen = jnp.take(weighted, source_slots[step], axis=1)
        picked = spread(chosen, "sta", owners[step])
        outputs.append(lax.psum(cross(picked, weighted, table), "win"))
    return jnp.stack(outputs)


def solution(mesh):
    small = mesh.shape["sta"] == 16 and mesh.shape["win"] == 2
    return jax.shard_map(
        on_device if small else on_device_general,
        mesh=mesh,
        in_specs=(P("win", "sta", None, None, None), P("win", "sta"), P(), P()),
        out_specs=P(None, None, None, "sta", None, None),
        check_vma=False,
    )
```

```python
import functools
import math

import jax
import jax.numpy as jnp
import numpy as np
from jax import lax
from jax.experimental import pallas as pl
from jax.experimental.pallas import tpu as pltpu
from jax.sharding import PartitionSpec as P

NLAG = 768
LANES = 128
MIB = 1024 * 1024


def lag_table(bins, lags, windows):
    freq = np.arange(bins, dtype=np.int64) + 360
    shift = np.arange(lags, dtype=np.int64) - lags // 2
    phase = np.mod(freq[:, None] * shift[None, :], 7200).astype(np.float32) * np.float32(
        2.0 * math.pi / 7200.0
    )
    scale = np.float32(1.0 / math.sqrt(windows * bins))
    real = (np.cos(phase) * scale).reshape(bins // LANES, 1, LANES, lags)
    imag = (-np.sin(phase) * scale).reshape(bins // LANES, 1, LANES, lags)
    return np.concatenate([real, imag], axis=1).reshape(2 * bins, lags).astype(jnp.bfloat16)


def whiten_kernel(flags_hbm, x_hbm, pieces_ref, rec_ref, flags, x_ref, sems):
    copies = (
        pltpu.make_async_copy(flags_hbm, flags, sems.at[0]),
        pltpu.make_async_copy(x_hbm, x_ref, sems.at[1]),
    )
    for copy in copies:
        copy.start()
    for copy in copies:
        copy.wait()
    wins, stas, comps, _, bins = x_ref.shape
    core = lax.axis_index("win")
    place = ((0, 1 + core), (2 - core, 3))
    tiles = bins // LANES
    lane = lax.broadcasted_iota(jnp.int32, (wins * stas, LANES), 1)
    left = lane < 64
    sums = []
    for w in range(wins):
        for s in range(stas):
            x = x_ref[w, s]
            sums.append(jnp.sum(jnp.sum(x * x, axis=0), axis=0, keepdims=True))
    power = jnp.concatenate(sums, axis=0)
    weight = jnp.concatenate(
        [
            jnp.full((1, LANES), flags[w, s].astype(jnp.float32), jnp.float32)
            for w in range(wins)
            for s in range(stas)
        ],
        axis=0,
    )
    scales = []
    for c in range(tiles):
        tile = power[:, c * LANES : (c + 1) * LANES]
        low = jnp.sum(jnp.where(left, tile, 0.0), axis=1, keepdims=True)
        high = jnp.sum(jnp.where(left, 0.0, tile), axis=1, keepdims=True)
        mean = jnp.where(left, low, high) * (1.0 / (64 * 2 * comps))
        scales.append(weight / jnp.sqrt(mean + 1e-06))
    scale = jnp.concatenate(scales, axis=1)
    for w in range(wins):
        for s in range(stas):
            k = w * stas + s
            weights = scale[k : k + 1]
            for i in range(comps):
                y = x_ref[w, s, i] * weights
                for part in range(2):
                    for copy in range(2):
                        row = pl.ds((copy * comps + i) * stas + s, 1)
                        rec_ref[w, part, row, :] = y[part : part + 1]
                    for c in range(tiles):
                        pieces_ref[4 * s + place[w][part], pl.ds(i * tiles + c, 1), :] = y[
                            part : part + 1, c * LANES : (c + 1) * LANES
                        ]
    rest = pieces_ref.shape[1] - comps * tiles
    if rest:
        for k in range(wins * stas * 2):
            pieces_ref[k, pl.ds(comps * tiles, rest), :] = jnp.zeros((rest, LANES), jnp.float32)


def whiten(spectra, flags):
    wins, stas, _, comps, bins = spectra.shape
    rows = -(-comps * (bins // LANES) // 8) * 8
    return pl.pallas_call(
        whiten_kernel,
        out_shape=(
            jax.ShapeDtypeStruct((wins * stas * 2, rows, LANES), jnp.float32),
            jax.ShapeDtypeStruct((wins, 2, 2 * comps * stas, bins), jnp.float32),
        ),
        in_specs=[pl.BlockSpec(memory_space=pltpu.HBM)] * 2,
        out_specs=(
            pl.BlockSpec(memory_space=pltpu.VMEM),
            pl.BlockSpec(memory_space=pltpu.VMEM),
        ),
        scratch_shapes=[
            pltpu.SMEM(flags.shape, jnp.int32),
            pltpu.VMEM((wins, stas, comps, 2, bins), jnp.float32),
            pltpu.SemaphoreType.DMA((2,)),
        ],
        compiler_params=pltpu.CompilerParams(vmem_limit_bytes=61 * MIB),
        name="whiten",
    )(flags, jnp.transpose(spectra, (0, 1, 3, 2, 4)))


def pick_kernel(params, got_ref, before, keep_ref, send_ref):
    half = keep_ref.shape[0]
    for t in range(half):
        keep_ref[t] = got_ref[params[t]]
        send_ref[t] = got_ref[params[half + t]]


def pick(params, got, before, steps):
    shape = jax.ShapeDtypeStruct((steps // 2,) + got.shape[1:], jnp.float32)
    smem = pl.BlockSpec(memory_space=pltpu.SMEM)
    vmem = pl.BlockSpec(memory_space=pltpu.VMEM)
    return pl.pallas_call(
        pick_kernel,
        out_shape=(shape, shape),
        in_specs=[smem, vmem, vmem],
        out_specs=(vmem, vmem),
        compiler_params=pltpu.CompilerParams(vmem_limit_bytes=8 * MIB),
        name="pick",
    )(params, got, before)


def pack_kernel(*refs, count):
    for n in range(count):
        refs[-1][n] = refs[n][...]


def pack(values, before):
    vmem = pl.BlockSpec(memory_space=pltpu.VMEM)
    return pl.pallas_call(
        functools.partial(pack_kernel, count=len(values)),
        out_shape=jax.ShapeDtypeStruct((len(values),) + values[0].shape, values[0].dtype),
        in_specs=[vmem] * (len(values) + len(before)),
        out_specs=vmem,
        compiler_params=pltpu.CompilerParams(vmem_limit_bytes=8 * MIB),
        name="pack",
    )(*values, *before)


def load_kernel(table_hbm, after, out_ref, sem):
    copy = pltpu.make_async_copy(table_hbm, out_ref, sem)
    copy.start()
    copy.wait()


def load(table, after):
    vmem = pl.BlockSpec(memory_space=pltpu.VMEM)
    return pl.pallas_call(
        load_kernel,
        out_shape=jax.ShapeDtypeStruct(table.shape, table.dtype),
        in_specs=[pl.BlockSpec(memory_space=pltpu.HBM), vmem],
        out_specs=vmem,
        scratch_shapes=[pltpu.SemaphoreType.DMA],
        compiler_params=pltpu.CompilerParams(vmem_limit_bytes=8 * MIB),
        cost_estimate=pl.CostEstimate(flops=0, bytes_accessed=5 * MIB, transcendentals=0),
        name="load",
    )(table, after)


def correlate_kernel(params, *refs, count):
    spots_in = [refs[n * count : (n + 1) * count] for n in range(4)]
    receivers_in, table, out_ref, lhs = refs[4 * count : 4 * count + 2], *refs[4 * count + 2 :]
    _, groups, steps, _, _ = spots_in[0][0].shape
    offsets = [(k, n) for k in range(count) for n in range(spots_in[0][k].shape[0])]
    depth = len(offsets)
    tiles = receivers_in[0].shape[3] // LANES
    place, core = lax.axis_index("sta") & 3, lax.axis_index("win")
    window, part = (place >> (1 - core)) & 1, (place >> core) & 1
    kinds = ((window, part), (part, window))
    signs = [1.0 - 2.0 * p.astype(jnp.float32) for _, p in kinds]
    spots = (((0, 1), (2, 3)), ((0, 2), (1, 3)))
    upper = lax.broadcasted_iota(jnp.int32, (8, LANES), 0) < 4

    def source(spot, g, n, c):
        t, (k, offset), i = n // (3 * depth), offsets[(n // 3) % depth], n % 3
        line = spots_in[spot][k][offset, g, t, pl.ds(i * tiles + c, 1), :]
        return jnp.broadcast_to(line, (8, LANES))

    def chunk(c, carry):
        lanes = pl.ds(pl.multiple_of(c * LANES, LANES), LANES)
        receivers = [
            [[receivers_in[g][kinds[g][0] ^ w, kinds[g][1] ^ p, :, lanes] for p in range(2)]
             for w in range(2)]
            for g in range(groups)
        ]
        for block in range(steps * depth * 3 // 4):
            real_tiles, imag_tiles = [], []
            for pair in range(2):
                numbers = (block * 4 + pair * 2, block * 4 + pair * 2 + 1)
                real = [0.0] * 3
                imag = [0.0] * 3
                for g in range(groups):
                    part_imag = [0.0] * 3
                    for w in range(2):
                        spread = []
                        for p in range(2):
                            rows = [source(spots[g][w][p], g, n, c) for n in numbers]
                            spread.append((rows[0], jnp.where(upper, rows[0], rows[1]), rows[1]))
                        for k in range(3):
                            ra = receivers[g][w][0][8 * k : 8 * k + 8]
                            rb = receivers[g][w][1][8 * k : 8 * k + 8]
                            a, b = spread[0][k], spread[1][k]
                            real[k] += a * ra + b * rb
                            part_imag[k] += b * ra - a * rb
                    for k in range(3):
                        imag[k] += signs[g] * part_imag[k]
                real_tiles += real
                imag_tiles += imag
            at = pl.ds(block * 48, 48)
            base = c * 2 * LANES
            lhs[at, pl.ds(pl.multiple_of(base, LANES), LANES)] = jnp.concatenate(
                real_tiles, axis=0
            ).astype(jnp.bfloat16)
            lhs[at, pl.ds(pl.multiple_of(base + LANES, LANES), LANES)] = jnp.concatenate(
                imag_tiles, axis=0
            ).astype(jnp.bfloat16)
        return carry

    lax.fori_loop(0, tiles, chunk, 0)
    for n in range(out_ref.shape[3] // 256):
        lags = pl.ds(n * 256, 256)
        result = jnp.dot(lhs[...], table[:, lags], preferred_element_type=jnp.float32)
        for t in range(steps):
            for offset in range(depth):
                first = params[2 * steps + depth * t + offset] * 9
                for k in range(9):
                    row = 4 * ((t * depth + offset) * 9 + k)
                    out_ref[t, first + k, :, lags] = result[row : row + 4]


def correlate(params, sources, own, other, table):
    count = len(sources[0])
    steps = sources[0][0].shape[2]
    depth = sum(value.shape[0] for value in sources[0])
    bins = own.shape[3]
    lags = table.shape[1]
    rows = steps * depth * 3 * 12
    vmem = pl.BlockSpec(memory_space=pltpu.VMEM)
    return pl.pallas_call(
        functools.partial(correlate_kernel, count=count),
        out_shape=jax.ShapeDtypeStruct((steps, depth * 9, 4, lags), jnp.float32),
        in_specs=[pl.BlockSpec(memory_space=pltpu.SMEM)] + [vmem] * (4 * count + 3),
        out_specs=vmem,
        scratch_shapes=[pltpu.VMEM((rows, 2 * bins), jnp.bfloat16)],
        compiler_params=pltpu.CompilerParams(vmem_limit_bytes=20 * MIB),
        cost_estimate=pl.CostEstimate(
            flops=4 * rows * bins * lags, bytes_accessed=8 * MIB, transcendentals=0
        ),
        name="correlate",
    )(params, *[value for spot in sources for value in spot], own, other, table)


def write_steps(half, out, core, sems):
    parts = sems.shape[1]
    size = half.shape[1] // parts
    copies = [
        pltpu.make_async_copy(
            half.at[t, pl.ds(n * size, size)],
            out.at[2 * t + core, pl.ds(n * size, size)],
            sems.at[t, n],
        )
        for t in range(half.shape[0])
        for n in range(parts)
    ]
    for copy in copies:
        copy.start()
    for copy in copies:
        copy.wait()


def put_kernel(own, out, sems):
    write_steps(own, out, lax.axis_index("win"), sems)


def put(own):
    return pl.pallas_call(
        put_kernel,
        out_shape=jax.ShapeDtypeStruct((2 * own.shape[0],) + own.shape[1:], own.dtype),
        in_specs=[pl.BlockSpec(memory_space=pltpu.VMEM)],
        out_specs=pl.BlockSpec(memory_space=pltpu.HBM),
        scratch_shapes=[pltpu.SemaphoreType.DMA((own.shape[0], 4))],
        compiler_params=pltpu.CompilerParams(vmem_limit_bytes=8 * MIB),
        name="put",
    )(own)


def join_kernel(other, whole, out, sems):
    write_steps(other, out, 1 - lax.axis_index("win"), sems)


def join(other, whole):
    hbm = pl.BlockSpec(memory_space=pltpu.HBM)
    return pl.pallas_call(
        join_kernel,
        out_shape=jax.ShapeDtypeStruct(whole.shape, whole.dtype),
        in_specs=[pl.BlockSpec(memory_space=pltpu.VMEM), hbm],
        out_specs=hbm,
        scratch_shapes=[pltpu.SemaphoreType.DMA((other.shape[0], 4))],
        input_output_aliases={1: 0},
        compiler_params=pltpu.CompilerParams(vmem_limit_bytes=8 * MIB),
        name="join",
    )(other, whole)


def swap(value):
    return lax.ppermute(value, "win", [(0, 1), (1, 0)])


def on_device(spectra, flags, owners, source_slots):
    wins, stas, _, comps, bins = spectra.shape
    steps, sources = source_slots.shape
    at = lax.axis_index("sta")
    core = lax.axis_index("win")
    blocks = lax.axis_size("sta")
    pairs = owners.reshape(steps // 2, 2)
    slots = source_slots.reshape(steps // 2, 2, sources)
    z = at >> 2
    mine = jnp.where(core == 0, slots[:, 0], slots[:, 1])
    held = z ^ jnp.arange(sources, dtype=jnp.int32)
    order = jnp.arange(sources, dtype=jnp.int32)
    found = jnp.sum(
        jnp.where(mine[:, None, :] == held[None, :, None], order[None, None, :], 0), axis=2
    )
    params = jnp.concatenate(
        [
            jnp.where(core == 0, pairs[:, 0], pairs[:, 1]),
            jnp.where(core == 0, pairs[:, 1], pairs[:, 0]),
            found.reshape(-1),
        ]
    ).astype(jnp.int32)
    pieces, own = whiten(spectra, flags)
    other = swap(own)
    got = lax.all_to_all(pieces, "sta", 0, 0)
    keep, send = pick(params, got, other, steps)
    mine = jnp.stack([keep, swap(send)])

    def partner(bits):
        return [(i, i ^ bits) for i in range(blocks)]

    def by_core(first, second):
        bits = (first, second)
        return [(2 * i + c, 2 * (i ^ bits[c]) + c) for i in range(blocks) for c in range(2)]

    def plane(value):
        near = lax.ppermute(value, ("sta", "win"), by_core(1, 2))
        side = lax.ppermute(value, ("sta", "win"), by_core(2, 1))
        return value, near, side, lax.ppermute(value, "sta", partner(3))

    far, farther = [lax.ppermute(mine, "sta", partner(4 * k)) for k in (2, 3)]
    first = plane(mine)
    second = [lax.ppermute(value, "sta", partner(4)) for value in first]
    rest = plane(pack((far, farther), first[1:]))
    sources_in = [(a[None], b[None], c) for a, b, c in zip(first, second, rest)]
    table = jnp.asarray(lag_table(bins, NLAG, wins * lax.axis_size("win")))
    table = load(table, mine)
    half = correlate(params, sources_in, own, other, table)
    whole = join(swap(half), put(half))
    return whole.reshape(steps, sources, comps, comps, stas, NLAG).transpose(0, 1, 2, 4, 3, 5)


def spread(value, axis, source):
    kept = jnp.where(lax.axis_index(axis) == source, value, 0).astype(value.dtype)
    return lax.psum(kept, axis)


def cross(picked, receivers, table):
    src_re = picked[:, :, 0][:, :, :, None, None, :]
    src_im = picked[:, :, 1][:, :, :, None, None, :]
    rec_re = receivers[:, :, 0][:, None, None, :, :, :]
    rec_im = receivers[:, :, 1][:, None, None, :, :, :]
    real = jnp.sum(src_re * rec_re + src_im * rec_im, axis=0)
    imag = jnp.sum(src_im * rec_re - src_re * rec_im, axis=0)
    shape = real.shape
    both = jnp.stack(
        [part.reshape(shape[:4] + (shape[4] // LANES, LANES)) for part in (real, imag)], axis=5
    )
    rows = both.reshape(-1, 2 * shape[4]).astype(jnp.bfloat16)
    lagged = jnp.dot(rows, table, preferred_element_type=jnp.float32)
    return lagged.reshape(shape[:4] + (table.shape[1],))


def on_device_general(spectra, flags, owners, source_slots):
    shape = spectra.shape
    blocks = spectra.reshape(shape[:4] + (shape[4] // 64, 64))
    power = jnp.mean(blocks * blocks, axis=(2, 3, 5), keepdims=True)
    whitened = (blocks / jnp.sqrt(power + 1e-06)).reshape(shape)
    weighted = whitened * flags.astype(jnp.float32)[:, :, None, None, None]
    table = jnp.asarray(lag_table(shape[4], NLAG, shape[0] * lax.axis_size("win")))
    outputs = []
    for step in range(source_slots.shape[0]):
        chosen = jnp.take(weighted, source_slots[step], axis=1)
        picked = spread(chosen, "sta", owners[step])
        outputs.append(lax.psum(cross(picked, weighted, table), "win"))
    return jnp.stack(outputs)


def solution(mesh):
    small = mesh.shape["sta"] == 16 and mesh.shape["win"] == 2
    return jax.shard_map(
        on_device if small else on_device_general,
        mesh=mesh,
        in_specs=(P("win", "sta", None, None, None), P("win", "sta"), P(), P()),
        out_specs=P(None, None, None, "sta", None, None),
        check_vma=False,
    )
```

```python
import functools
import math

import jax
import jax.numpy as jnp
import numpy as np
from jax import lax
from jax.experimental import pallas as pl
from jax.experimental.pallas import tpu as pltpu
from jax.sharding import PartitionSpec as P

NLAG = 768
LANES = 128
MIB = 1024 * 1024


def lag_table(bins, lags, windows):
    freq = np.arange(bins, dtype=np.int64) + 360
    shift = np.arange(lags, dtype=np.int64) - lags // 2
    phase = np.mod(freq[:, None] * shift[None, :], 7200).astype(np.float32) * np.float32(
        2.0 * math.pi / 7200.0
    )
    scale = np.float32(1.0 / math.sqrt(windows * bins))
    real = (np.cos(phase) * scale).reshape(bins // LANES, 1, LANES, lags)
    imag = (-np.sin(phase) * scale).reshape(bins // LANES, 1, LANES, lags)
    return np.concatenate([real, imag], axis=1).reshape(2 * bins, lags).astype(jnp.bfloat16)


def whiten_kernel(flags_hbm, x_hbm, pieces_ref, rec_ref, flags, x_ref, sems):
    copies = (
        pltpu.make_async_copy(flags_hbm, flags, sems.at[0]),
        pltpu.make_async_copy(x_hbm, x_ref, sems.at[1]),
    )
    for copy in copies:
        copy.start()
    for copy in copies:
        copy.wait()
    wins, stas, comps, _, bins = x_ref.shape
    core = lax.axis_index("win")
    place = ((0, 1 + core), (2 - core, 3))
    tiles = bins // LANES
    lane = lax.broadcasted_iota(jnp.int32, (wins * stas, LANES), 1)
    left = lane < 64
    sums = []
    for w in range(wins):
        for s in range(stas):
            x = x_ref[w, s]
            sums.append(jnp.sum(jnp.sum(x * x, axis=0), axis=0, keepdims=True))
    power = jnp.concatenate(sums, axis=0)
    weight = jnp.concatenate(
        [
            jnp.full((1, LANES), flags[w, s].astype(jnp.float32), jnp.float32)
            for w in range(wins)
            for s in range(stas)
        ],
        axis=0,
    )
    scales = []
    for c in range(tiles):
        tile = power[:, c * LANES : (c + 1) * LANES]
        low = jnp.sum(jnp.where(left, tile, 0.0), axis=1, keepdims=True)
        high = jnp.sum(jnp.where(left, 0.0, tile), axis=1, keepdims=True)
        mean = jnp.where(left, low, high) * (1.0 / (64 * 2 * comps))
        scales.append(weight / jnp.sqrt(mean + 1e-06))
    scale = jnp.concatenate(scales, axis=1)
    for w in range(wins):
        for s in range(stas):
            k = w * stas + s
            weights = scale[k : k + 1]
            for i in range(comps):
                y = x_ref[w, s, i] * weights
                for part in range(2):
                    for copy in range(2):
                        row = pl.ds((copy * comps + i) * stas + s, 1)
                        rec_ref[w, part, row, :] = y[part : part + 1]
                    for c in range(tiles):
                        pieces_ref[4 * s + place[w][part], pl.ds(i * tiles + c, 1), :] = y[
                            part : part + 1, c * LANES : (c + 1) * LANES
                        ]
    rest = pieces_ref.shape[1] - comps * tiles
    if rest:
        for k in range(wins * stas * 2):
            pieces_ref[k, pl.ds(comps * tiles, rest), :] = jnp.zeros((rest, LANES), jnp.float32)


def whiten(spectra, flags):
    wins, stas, _, comps, bins = spectra.shape
    rows = -(-comps * (bins // LANES) // 8) * 8
    return pl.pallas_call(
        whiten_kernel,
        out_shape=(
            jax.ShapeDtypeStruct((wins * stas * 2, rows, LANES), jnp.float32),
            jax.ShapeDtypeStruct((wins, 2, 2 * comps * stas, bins), jnp.float32),
        ),
        in_specs=[pl.BlockSpec(memory_space=pltpu.HBM)] * 2,
        out_specs=(
            pl.BlockSpec(memory_space=pltpu.VMEM),
            pl.BlockSpec(memory_space=pltpu.VMEM),
        ),
        scratch_shapes=[
            pltpu.SMEM(flags.shape, jnp.int32),
            pltpu.VMEM((wins, stas, comps, 2, bins), jnp.float32),
            pltpu.SemaphoreType.DMA((2,)),
        ],
        compiler_params=pltpu.CompilerParams(vmem_limit_bytes=61 * MIB),
        name="whiten",
    )(flags, jnp.transpose(spectra, (0, 1, 3, 2, 4)))


def pick_kernel(params, got_ref, before, keep_ref, send_ref):
    half = keep_ref.shape[0]
    for t in range(half):
        keep_ref[t] = got_ref[params[t]]
        send_ref[t] = got_ref[params[half + t]]


def pick(params, got, before, steps):
    shape = jax.ShapeDtypeStruct((steps // 2,) + got.shape[1:], jnp.float32)
    smem = pl.BlockSpec(memory_space=pltpu.SMEM)
    vmem = pl.BlockSpec(memory_space=pltpu.VMEM)
    return pl.pallas_call(
        pick_kernel,
        out_shape=(shape, shape),
        in_specs=[smem, vmem, vmem],
        out_specs=(vmem, vmem),
        compiler_params=pltpu.CompilerParams(vmem_limit_bytes=8 * MIB),
        name="pick",
    )(params, got, before)


def pack_kernel(*refs, count):
    for n, value in enumerate(refs[-1 - count : -1]):
        refs[-1][n] = value[...]


def pack(values, before):
    vmem = pl.BlockSpec(memory_space=pltpu.VMEM)
    return pl.pallas_call(
        functools.partial(pack_kernel, count=len(values)),
        out_shape=jax.ShapeDtypeStruct((len(values),) + values[0].shape, values[0].dtype),
        in_specs=[vmem] * (len(values) + len(before)),
        out_specs=vmem,
        compiler_params=pltpu.CompilerParams(vmem_limit_bytes=8 * MIB),
        name="pack",
    )(*before, *values)


def load_kernel(table_hbm, after, out_ref, sem):
    copy = pltpu.make_async_copy(table_hbm, out_ref, sem)
    copy.start()
    copy.wait()


def load(table, after):
    vmem = pl.BlockSpec(memory_space=pltpu.VMEM)
    return pl.pallas_call(
        load_kernel,
        out_shape=jax.ShapeDtypeStruct(table.shape, table.dtype),
        in_specs=[pl.BlockSpec(memory_space=pltpu.HBM), vmem],
        out_specs=vmem,
        scratch_shapes=[pltpu.SemaphoreType.DMA],
        compiler_params=pltpu.CompilerParams(vmem_limit_bytes=8 * MIB),
        cost_estimate=pl.CostEstimate(flops=0, bytes_accessed=5 * MIB, transcendentals=0),
        name="load",
    )(table, after)


def correlate_kernel(params, *refs, count):
    spots_in = [refs[n * count : (n + 1) * count] for n in range(4)]
    receivers_in, table, out_ref, lhs = refs[4 * count : 4 * count + 2], *refs[4 * count + 2 :]
    _, groups, steps, _, _ = spots_in[0][0].shape
    offsets = [(k, n) for k in range(count) for n in range(spots_in[0][k].shape[0])]
    depth = len(offsets)
    tiles = receivers_in[0].shape[3] // LANES
    place, core = lax.axis_index("sta") & 3, lax.axis_index("win")
    window, part = (place >> (1 - core)) & 1, (place >> core) & 1
    kinds = ((window, part), (part, window))
    signs = [1.0 - 2.0 * p.astype(jnp.float32) for _, p in kinds]
    spots = (((0, 1), (2, 3)), ((0, 2), (1, 3)))
    upper = lax.broadcasted_iota(jnp.int32, (8, LANES), 0) < 4

    def source(spot, g, n, c):
        t, (k, offset), i = n // (3 * depth), offsets[(n // 3) % depth], n % 3
        line = spots_in[spot][k][offset, g, t, pl.ds(i * tiles + c, 1), :]
        return jnp.broadcast_to(line, (8, LANES))

    def chunk(c, carry):
        lanes = pl.ds(pl.multiple_of(c * LANES, LANES), LANES)
        receivers = [
            [[receivers_in[g][kinds[g][0] ^ w, kinds[g][1] ^ p, :, lanes] for p in range(2)]
             for w in range(2)]
            for g in range(groups)
        ]
        for block in range(steps * depth * 3 // 4):
            real_tiles, imag_tiles = [], []
            for pair in range(2):
                numbers = (block * 4 + pair * 2, block * 4 + pair * 2 + 1)
                real = [0.0] * 3
                imag = [0.0] * 3
                for g in range(groups):
                    part_imag = [0.0] * 3
                    for w in range(2):
                        spread = []
                        for p in range(2):
                            rows = [source(spots[g][w][p], g, n, c) for n in numbers]
                            spread.append((rows[0], jnp.where(upper, rows[0], rows[1]), rows[1]))
                        for k in range(3):
                            ra = receivers[g][w][0][8 * k : 8 * k + 8]
                            rb = receivers[g][w][1][8 * k : 8 * k + 8]
                            a, b = spread[0][k], spread[1][k]
                            real[k] += a * ra + b * rb
                            part_imag[k] += b * ra - a * rb
                    for k in range(3):
                        imag[k] += signs[g] * part_imag[k]
                real_tiles += real
                imag_tiles += imag
            at = pl.ds(block * 48, 48)
            base = c * 2 * LANES
            lhs[at, pl.ds(pl.multiple_of(base, LANES), LANES)] = jnp.concatenate(
                real_tiles, axis=0
            ).astype(jnp.bfloat16)
            lhs[at, pl.ds(pl.multiple_of(base + LANES, LANES), LANES)] = jnp.concatenate(
                imag_tiles, axis=0
            ).astype(jnp.bfloat16)
        return carry

    lax.fori_loop(0, tiles, chunk, 0)
    for n in range(out_ref.shape[3] // 256):
        lags = pl.ds(n * 256, 256)
        result = jnp.dot(lhs[...], table[:, lags], preferred_element_type=jnp.float32)
        for t in range(steps):
            for offset in range(depth):
                first = params[2 * steps + depth * t + offset] * 9
                for k in range(9):
                    row = 4 * ((t * depth + offset) * 9 + k)
                    out_ref[t, first + k, :, lags] = result[row : row + 4]


def correlate(params, sources, own, other, table):
    count = len(sources[0])
    steps = sources[0][0].shape[2]
    depth = sum(value.shape[0] for value in sources[0])
    bins = own.shape[3]
    lags = table.shape[1]
    rows = steps * depth * 3 * 12
    vmem = pl.BlockSpec(memory_space=pltpu.VMEM)
    return pl.pallas_call(
        functools.partial(correlate_kernel, count=count),
        out_shape=jax.ShapeDtypeStruct((steps, depth * 9, 4, lags), jnp.float32),
        in_specs=[pl.BlockSpec(memory_space=pltpu.SMEM)] + [vmem] * (4 * count + 3),
        out_specs=vmem,
        scratch_shapes=[pltpu.VMEM((rows, 2 * bins), jnp.bfloat16)],
        compiler_params=pltpu.CompilerParams(vmem_limit_bytes=20 * MIB),
        cost_estimate=pl.CostEstimate(
            flops=4 * rows * bins * lags, bytes_accessed=8 * MIB, transcendentals=0
        ),
        name="correlate",
    )(params, *[value for spot in sources for value in spot], own, other, table)


def write_steps(half, out, core, sems):
    parts = sems.shape[1]
    size = half.shape[1] // parts
    copies = [
        pltpu.make_async_copy(
            half.at[t, pl.ds(n * size, size)],
            out.at[2 * t + core, pl.ds(n * size, size)],
            sems.at[t, n],
        )
        for t in range(half.shape[0])
        for n in range(parts)
    ]
    for copy in copies:
        copy.start()
    for copy in copies:
        copy.wait()


def put_kernel(own, out, sems):
    write_steps(own, out, lax.axis_index("win"), sems)


def put(own):
    return pl.pallas_call(
        put_kernel,
        out_shape=jax.ShapeDtypeStruct((2 * own.shape[0],) + own.shape[1:], own.dtype),
        in_specs=[pl.BlockSpec(memory_space=pltpu.VMEM)],
        out_specs=pl.BlockSpec(memory_space=pltpu.HBM),
        scratch_shapes=[pltpu.SemaphoreType.DMA((own.shape[0], 4))],
        compiler_params=pltpu.CompilerParams(vmem_limit_bytes=8 * MIB),
        name="put",
    )(own)


def join_kernel(other, whole, out, sems):
    write_steps(other, out, 1 - lax.axis_index("win"), sems)


def join(other, whole):
    hbm = pl.BlockSpec(memory_space=pltpu.HBM)
    return pl.pallas_call(
        join_kernel,
        out_shape=jax.ShapeDtypeStruct(whole.shape, whole.dtype),
        in_specs=[pl.BlockSpec(memory_space=pltpu.VMEM), hbm],
        out_specs=hbm,
        scratch_shapes=[pltpu.SemaphoreType.DMA((other.shape[0], 4))],
        input_output_aliases={1: 0},
        compiler_params=pltpu.CompilerParams(vmem_limit_bytes=8 * MIB),
        name="join",
    )(other, whole)


def swap(value):
    return lax.ppermute(value, "win", [(0, 1), (1, 0)])


def on_device(spectra, flags, owners, source_slots):
    wins, stas, _, comps, bins = spectra.shape
    steps, sources = source_slots.shape
    at = lax.axis_index("sta")
    core = lax.axis_index("win")
    blocks = lax.axis_size("sta")
    pairs = owners.reshape(steps // 2, 2)
    slots = source_slots.reshape(steps // 2, 2, sources)
    z = at >> 2
    mine = jnp.where(core == 0, slots[:, 0], slots[:, 1])
    held = z ^ jnp.arange(sources, dtype=jnp.int32)
    order = jnp.arange(sources, dtype=jnp.int32)
    found = jnp.sum(
        jnp.where(mine[:, None, :] == held[None, :, None], order[None, None, :], 0), axis=2
    )
    params = jnp.concatenate(
        [
            jnp.where(core == 0, pairs[:, 0], pairs[:, 1]),
            jnp.where(core == 0, pairs[:, 1], pairs[:, 0]),
            found.reshape(-1),
        ]
    ).astype(jnp.int32)
    pieces, own = whiten(spectra, flags)
    other = swap(own)
    got = lax.all_to_all(pieces, "sta", 0, 0)
    keep, send = pick(params, got, other, steps)
    mine = jnp.stack([keep, swap(send)])

    def partner(bits):
        return [(i, i ^ bits) for i in range(blocks)]

    def by_core(first, second):
        bits = (first, second)
        return [(2 * i + c, 2 * (i ^ bits[c]) + c) for i in range(blocks) for c in range(2)]

    def plane(value):
        near = lax.ppermute(value, ("sta", "win"), by_core(1, 2))
        side = lax.ppermute(value, ("sta", "win"), by_core(2, 1))
        return value, near, side, lax.ppermute(value, "sta", partner(3))

    first = plane(mine)
    far, farther = [lax.ppermute(mine, "sta", partner(4 * k)) for k in (2, 3)]
    second = [lax.ppermute(value, "sta", partner(4)) for value in first]
    table = load(jnp.asarray(lag_table(bins, NLAG, wins * lax.axis_size("win"))), mine)
    rest = plane(pack((far, farther), (*first[1:], table)))
    sources_in = [(a[None], b[None], c) for a, b, c in zip(first, second, rest)]
    half = correlate(params, sources_in, own, other, table)
    whole = join(swap(half), put(half))
    return whole.reshape(steps, sources, comps, comps, stas, NLAG).transpose(0, 1, 2, 4, 3, 5)


def spread(value, axis, source):
    kept = jnp.where(lax.axis_index(axis) == source, value, 0).astype(value.dtype)
    return lax.psum(kept, axis)


def cross(picked, receivers, table):
    src_re = picked[:, :, 0][:, :, :, None, None, :]
    src_im = picked[:, :, 1][:, :, :, None, None, :]
    rec_re = receivers[:, :, 0][:, None, None, :, :, :]
    rec_im = receivers[:, :, 1][:, None, None, :, :, :]
    real = jnp.sum(src_re * rec_re + src_im * rec_im, axis=0)
    imag = jnp.sum(src_im * rec_re - src_re * rec_im, axis=0)
    shape = real.shape
    both = jnp.stack(
        [part.reshape(shape[:4] + (shape[4] // LANES, LANES)) for part in (real, imag)], axis=5
    )
    rows = both.reshape(-1, 2 * shape[4]).astype(jnp.bfloat16)
    lagged = jnp.dot(rows, table, preferred_element_type=jnp.float32)
    return lagged.reshape(shape[:4] + (table.shape[1],))


def on_device_general(spectra, flags, owners, source_slots):
    shape = spectra.shape
    blocks = spectra.reshape(shape[:4] + (shape[4] // 64, 64))
    power = jnp.mean(blocks * blocks, axis=(2, 3, 5), keepdims=True)
    whitened = (blocks / jnp.sqrt(power + 1e-06)).reshape(shape)
    weighted = whitened * flags.astype(jnp.float32)[:, :, None, None, None]
    table = jnp.asarray(lag_table(shape[4], NLAG, shape[0] * lax.axis_size("win")))
    outputs = []
    for step in range(source_slots.shape[0]):
        chosen = jnp.take(weighted, source_slots[step], axis=1)
        picked = spread(chosen, "sta", owners[step])
        outputs.append(lax.psum(cross(picked, weighted, table), "win"))
    return jnp.stack(outputs)


def solution(mesh):
    small = mesh.shape["sta"] == 16 and mesh.shape["win"] == 2
    return jax.shard_map(
        on_device if small else on_device_general,
        mesh=mesh,
        in_specs=(P("win", "sta", None, None, None), P("win", "sta"), P(), P()),
        out_specs=P(None, None, None, "sta", None, None),
        check_vma=False,
    )
```

```python
import functools
import math

import jax
import jax.numpy as jnp
import numpy as np
from jax import lax
from jax.experimental import pallas as pl
from jax.experimental.pallas import tpu as pltpu
from jax.sharding import PartitionSpec as P

NLAG = 768
LANES = 128
MIB = 1024 * 1024


def lag_table(bins, lags, windows):
    freq = np.arange(bins, dtype=np.int64) + 360
    shift = np.arange(lags, dtype=np.int64) - lags // 2
    phase = np.mod(freq[:, None] * shift[None, :], 7200).astype(np.float32) * np.float32(
        2.0 * math.pi / 7200.0
    )
    scale = np.float32(1.0 / math.sqrt(windows * bins))
    real = (np.cos(phase) * scale).reshape(bins // LANES, 1, LANES, lags)
    imag = (-np.sin(phase) * scale).reshape(bins // LANES, 1, LANES, lags)
    return np.concatenate([real, imag], axis=1).reshape(2 * bins, lags).astype(jnp.bfloat16)


def whiten_kernel(flags_hbm, x_hbm, pieces_ref, rec_ref, flags, x_ref, sems):
    copies = (
        pltpu.make_async_copy(flags_hbm, flags, sems.at[0]),
        pltpu.make_async_copy(x_hbm, x_ref, sems.at[1]),
    )
    for copy in copies:
        copy.start()
    for copy in copies:
        copy.wait()
    wins, stas, comps, _, bins = x_ref.shape
    core = lax.axis_index("win")
    place = ((0, 1 + core), (2 - core, 3))
    tiles = bins // LANES
    lane = lax.broadcasted_iota(jnp.int32, (wins * stas, LANES), 1)
    left = lane < 64
    sums = []
    for w in range(wins):
        for s in range(stas):
            x = x_ref[w, s]
            sums.append(jnp.sum(jnp.sum(x * x, axis=0), axis=0, keepdims=True))
    power = jnp.concatenate(sums, axis=0)
    weight = jnp.concatenate(
        [
            jnp.full((1, LANES), flags[w, s].astype(jnp.float32), jnp.float32)
            for w in range(wins)
            for s in range(stas)
        ],
        axis=0,
    )
    scales = []
    for c in range(tiles):
        tile = power[:, c * LANES : (c + 1) * LANES]
        low = jnp.sum(jnp.where(left, tile, 0.0), axis=1, keepdims=True)
        high = jnp.sum(jnp.where(left, 0.0, tile), axis=1, keepdims=True)
        mean = jnp.where(left, low, high) * (1.0 / (64 * 2 * comps))
        scales.append(weight / jnp.sqrt(mean + 1e-06))
    scale = jnp.concatenate(scales, axis=1)
    for w in range(wins):
        for s in range(stas):
            k = w * stas + s
            weights = scale[k : k + 1]
            for i in range(comps):
                y = x_ref[w, s, i] * weights
                for part in range(2):
                    rec_ref[w, part, pl.ds(i * stas + s, 1), :] = y[part : part + 1]
                    for c in range(tiles):
                        pieces_ref[4 * s + place[w][part], pl.ds(i * tiles + c, 1), :] = y[
                            part : part + 1, c * LANES : (c + 1) * LANES
                        ]
    rest = pieces_ref.shape[1] - comps * tiles
    if rest:
        for k in range(wins * stas * 2):
            pieces_ref[k, pl.ds(comps * tiles, rest), :] = jnp.zeros((rest, LANES), jnp.float32)
    spare = rec_ref.shape[2] - comps * stas
    if spare:
        for w in range(wins):
            for part in range(2):
                rec_ref[w, part, pl.ds(comps * stas, spare), :] = jnp.zeros(
                    (spare, bins), jnp.float32
                )


def whiten(spectra, flags):
    wins, stas, _, comps, bins = spectra.shape
    rows = -(-comps * (bins // LANES) // 8) * 8
    recs = -(-comps * stas // 8) * 8
    return pl.pallas_call(
        whiten_kernel,
        out_shape=(
            jax.ShapeDtypeStruct((wins * stas * 2, rows, LANES), jnp.float32),
            jax.ShapeDtypeStruct((wins, 2, recs, bins), jnp.float32),
        ),
        in_specs=[pl.BlockSpec(memory_space=pltpu.HBM)] * 2,
        out_specs=(
            pl.BlockSpec(memory_space=pltpu.VMEM),
            pl.BlockSpec(memory_space=pltpu.VMEM),
        ),
        scratch_shapes=[
            pltpu.SMEM(flags.shape, jnp.int32),
            pltpu.VMEM((wins, stas, comps, 2, bins), jnp.float32),
            pltpu.SemaphoreType.DMA((2,)),
        ],
        compiler_params=pltpu.CompilerParams(vmem_limit_bytes=61 * MIB),
        name="whiten",
    )(flags, jnp.transpose(spectra, (0, 1, 3, 2, 4)))


def pick_kernel(params, got_ref, before, keep_ref, send_ref):
    half = keep_ref.shape[0]
    for t in range(half):
        keep_ref[t] = got_ref[params[t]]
        send_ref[t] = got_ref[params[half + t]]


def pick(params, got, before, steps):
    shape = jax.ShapeDtypeStruct((steps // 2,) + got.shape[1:], jnp.float32)
    smem = pl.BlockSpec(memory_space=pltpu.SMEM)
    vmem = pl.BlockSpec(memory_space=pltpu.VMEM)
    return pl.pallas_call(
        pick_kernel,
        out_shape=(shape, shape),
        in_specs=[smem, vmem, vmem],
        out_specs=(vmem, vmem),
        compiler_params=pltpu.CompilerParams(vmem_limit_bytes=8 * MIB),
        name="pick",
    )(params, got, before)


def pack_kernel(*refs, count):
    for n, value in enumerate(refs[-1 - count : -1]):
        refs[-1][n] = value[...]


def pack(values, before):
    vmem = pl.BlockSpec(memory_space=pltpu.VMEM)
    return pl.pallas_call(
        functools.partial(pack_kernel, count=len(values)),
        out_shape=jax.ShapeDtypeStruct((len(values),) + values[0].shape, values[0].dtype),
        in_specs=[vmem] * (len(values) + len(before)),
        out_specs=vmem,
        compiler_params=pltpu.CompilerParams(vmem_limit_bytes=8 * MIB),
        name="pack",
    )(*before, *values)


def load_kernel(table_hbm, after, out_ref, sem):
    copy = pltpu.make_async_copy(table_hbm, out_ref, sem)
    copy.start()
    copy.wait()


def load(table, after):
    vmem = pl.BlockSpec(memory_space=pltpu.VMEM)
    return pl.pallas_call(
        load_kernel,
        out_shape=jax.ShapeDtypeStruct(table.shape, table.dtype),
        in_specs=[pl.BlockSpec(memory_space=pltpu.HBM), vmem],
        out_specs=vmem,
        scratch_shapes=[pltpu.SemaphoreType.DMA],
        compiler_params=pltpu.CompilerParams(vmem_limit_bytes=8 * MIB),
        cost_estimate=pl.CostEstimate(flops=0, bytes_accessed=5 * MIB, transcendentals=0),
        name="load",
    )(table, after)


def correlate_kernel(params, *refs, count):
    spots_in = [refs[n * count : (n + 1) * count] for n in range(4)]
    receivers_in, table, out_ref, lhs, rec = (
        refs[4 * count : 4 * count + 2],
        *refs[4 * count + 2 :],
    )
    _, groups, steps, _, _ = spots_in[0][0].shape
    offsets = [(k, n) for k in range(count) for n in range(spots_in[0][k].shape[0])]
    depth = len(offsets)
    tiles = receivers_in[0].shape[3] // LANES
    place, core = lax.axis_index("sta") & 3, lax.axis_index("win")
    window, part = (place >> (1 - core)) & 1, (place >> core) & 1
    kinds = ((window, part), (part, window))
    signs = [1.0 - 2.0 * p.astype(jnp.float32) for _, p in kinds]
    for g in range(groups):
        for w in range(2):
            for p in range(2):
                rows = receivers_in[g][kinds[g][0] ^ w, kinds[g][1] ^ p, 0:12, :]
                rec[g, w, p, 0:12, :] = rows
                rec[g, w, p, 12:24, :] = rows
    spots = (((0, 1), (2, 3)), ((0, 2), (1, 3)))
    upper = lax.broadcasted_iota(jnp.int32, (8, LANES), 0) < 4

    def source(spot, g, n, c):
        t, (k, offset), i = n // (3 * depth), offsets[(n // 3) % depth], n % 3
        line = spots_in[spot][k][offset, g, t, pl.ds(i * tiles + c, 1), :]
        return jnp.broadcast_to(line, (8, LANES))

    def chunk(c, carry):
        lanes = pl.ds(pl.multiple_of(c * LANES, LANES), LANES)
        receivers = [
            [[rec[g, w, p, :, lanes] for p in range(2)] for w in range(2)] for g in range(groups)
        ]
        for block in range(steps * depth * 3 // 4):
            real_tiles, imag_tiles = [], []
            for pair in range(2):
                numbers = (block * 4 + pair * 2, block * 4 + pair * 2 + 1)
                real = [0.0] * 3
                imag = [0.0] * 3
                for g in range(groups):
                    part_imag = [0.0] * 3
                    for w in range(2):
                        spread = []
                        for p in range(2):
                            rows = [source(spots[g][w][p], g, n, c) for n in numbers]
                            spread.append((rows[0], jnp.where(upper, rows[0], rows[1]), rows[1]))
                        for k in range(3):
                            ra = receivers[g][w][0][8 * k : 8 * k + 8]
                            rb = receivers[g][w][1][8 * k : 8 * k + 8]
                            a, b = spread[0][k], spread[1][k]
                            real[k] += a * ra + b * rb
                            part_imag[k] += b * ra - a * rb
                    for k in range(3):
                        imag[k] += signs[g] * part_imag[k]
                real_tiles += real
                imag_tiles += imag
            at = pl.ds(block * 48, 48)
            base = c * 2 * LANES
            lhs[at, pl.ds(pl.multiple_of(base, LANES), LANES)] = jnp.concatenate(
                real_tiles, axis=0
            ).astype(jnp.bfloat16)
            lhs[at, pl.ds(pl.multiple_of(base + LANES, LANES), LANES)] = jnp.concatenate(
                imag_tiles, axis=0
            ).astype(jnp.bfloat16)
        return carry

    lax.fori_loop(0, tiles, chunk, 0, unroll=True)
    for n in range(out_ref.shape[3] // 256):
        lags = pl.ds(n * 256, 256)
        result = jnp.dot(lhs[...], table[:, lags], preferred_element_type=jnp.float32)
        for t in range(steps):
            for offset in range(depth):
                first = params[2 * steps + depth * t + offset] * 9
                for k in range(9):
                    row = 4 * ((t * depth + offset) * 9 + k)
                    out_ref[t, first + k, :, lags] = result[row : row + 4]


def correlate(params, sources, own, other, table):
    count = len(sources[0])
    steps = sources[0][0].shape[2]
    depth = sum(value.shape[0] for value in sources[0])
    bins = own.shape[3]
    lags = table.shape[1]
    rows = steps * depth * 3 * 12
    vmem = pl.BlockSpec(memory_space=pltpu.VMEM)
    return pl.pallas_call(
        functools.partial(correlate_kernel, count=count),
        out_shape=jax.ShapeDtypeStruct((steps, depth * 9, 4, lags), jnp.float32),
        in_specs=[pl.BlockSpec(memory_space=pltpu.SMEM)] + [vmem] * (4 * count + 3),
        out_specs=vmem,
        scratch_shapes=[
            pltpu.VMEM((rows, 2 * bins), jnp.bfloat16),
            pltpu.VMEM((2, 2, 2, 24, bins), jnp.float32),
        ],
        compiler_params=pltpu.CompilerParams(vmem_limit_bytes=20 * MIB),
        cost_estimate=pl.CostEstimate(
            flops=4 * rows * bins * lags, bytes_accessed=8 * MIB, transcendentals=0
        ),
        name="correlate",
    )(params, *[value for spot in sources for value in spot], own, other, table)


def write_steps(half, out, core, sems):
    parts = sems.shape[1]
    size = half.shape[1] // parts
    copies = [
        pltpu.make_async_copy(
            half.at[t, pl.ds(n * size, size)],
            out.at[2 * t + core, pl.ds(n * size, size)],
            sems.at[t, n],
        )
        for t in range(half.shape[0])
        for n in range(parts)
    ]
    for copy in copies:
        copy.start()
    for copy in copies:
        copy.wait()


def put_kernel(own, out, sems):
    write_steps(own, out, lax.axis_index("win"), sems)


def put(own):
    return pl.pallas_call(
        put_kernel,
        out_shape=jax.ShapeDtypeStruct((2 * own.shape[0],) + own.shape[1:], own.dtype),
        in_specs=[pl.BlockSpec(memory_space=pltpu.VMEM)],
        out_specs=pl.BlockSpec(memory_space=pltpu.HBM),
        scratch_shapes=[pltpu.SemaphoreType.DMA((own.shape[0], 4))],
        compiler_params=pltpu.CompilerParams(vmem_limit_bytes=8 * MIB),
        name="put",
    )(own)


def join_kernel(other, whole, out, sems):
    write_steps(other, out, 1 - lax.axis_index("win"), sems)


def join(other, whole):
    hbm = pl.BlockSpec(memory_space=pltpu.HBM)
    return pl.pallas_call(
        join_kernel,
        out_shape=jax.ShapeDtypeStruct(whole.shape, whole.dtype),
        in_specs=[pl.BlockSpec(memory_space=pltpu.VMEM), hbm],
        out_specs=hbm,
        scratch_shapes=[pltpu.SemaphoreType.DMA((other.shape[0], 4))],
        input_output_aliases={1: 0},
        compiler_params=pltpu.CompilerParams(vmem_limit_bytes=8 * MIB),
        name="join",
    )(other, whole)


def swap(value):
    return lax.ppermute(value, "win", [(0, 1), (1, 0)])


def on_device(spectra, flags, owners, source_slots):
    wins, stas, _, comps, bins = spectra.shape
    steps, sources = source_slots.shape
    at = lax.axis_index("sta")
    core = lax.axis_index("win")
    blocks = lax.axis_size("sta")
    pairs = owners.reshape(steps // 2, 2)
    slots = source_slots.reshape(steps // 2, 2, sources)
    z = at >> 2
    mine = jnp.where(core == 0, slots[:, 0], slots[:, 1])
    held = z ^ jnp.arange(sources, dtype=jnp.int32)
    order = jnp.arange(sources, dtype=jnp.int32)
    found = jnp.sum(
        jnp.where(mine[:, None, :] == held[None, :, None], order[None, None, :], 0), axis=2
    )
    params = jnp.concatenate(
        [
            jnp.where(core == 0, pairs[:, 0], pairs[:, 1]),
            jnp.where(core == 0, pairs[:, 1], pairs[:, 0]),
            found.reshape(-1),
        ]
    ).astype(jnp.int32)
    pieces, own = whiten(spectra, flags)
    other = swap(own)
    got = lax.all_to_all(pieces, "sta", 0, 0)
    keep, send = pick(params, got, other, steps)
    mine = jnp.stack([keep, swap(send)])

    def partner(bits):
        return [(i, i ^ bits) for i in range(blocks)]

    def by_core(first, second):
        bits = (first, second)
        return [(2 * i + c, 2 * (i ^ bits[c]) + c) for i in range(blocks) for c in range(2)]

    def plane(value):
        near = lax.ppermute(value, ("sta", "win"), by_core(1, 2))
        side = lax.ppermute(value, ("sta", "win"), by_core(2, 1))
        return value, near, side, lax.ppermute(value, "sta", partner(3))

    first = plane(mine)
    far, farther = [lax.ppermute(mine, "sta", partner(4 * k)) for k in (2, 3)]
    second = [lax.ppermute(value, "sta", partner(4)) for value in first]
    packed = pack((far, farther), first[1:])
    rest = plane(packed)
    table = load(jnp.asarray(lag_table(bins, NLAG, wins * lax.axis_size("win"))), packed)
    sources_in = [(a[None], b[None], c) for a, b, c in zip(first, second, rest)]
    half = correlate(params, sources_in, own, other, table)
    whole = join(swap(half), put(half))
    return whole.reshape(steps, sources, comps, comps, stas, NLAG).transpose(0, 1, 2, 4, 3, 5)


def spread(value, axis, source):
    kept = jnp.where(lax.axis_index(axis) == source, value, 0).astype(value.dtype)
    return lax.psum(kept, axis)


def cross(picked, receivers, table):
    src_re = picked[:, :, 0][:, :, :, None, None, :]
    src_im = picked[:, :, 1][:, :, :, None, None, :]
    rec_re = receivers[:, :, 0][:, None, None, :, :, :]
    rec_im = receivers[:, :, 1][:, None, None, :, :, :]
    real = jnp.sum(src_re * rec_re + src_im * rec_im, axis=0)
    imag = jnp.sum(src_im * rec_re - src_re * rec_im, axis=0)
    shape = real.shape
    both = jnp.stack(
        [part.reshape(shape[:4] + (shape[4] // LANES, LANES)) for part in (real, imag)], axis=5
    )
    rows = both.reshape(-1, 2 * shape[4]).astype(jnp.bfloat16)
    lagged = jnp.dot(rows, table, preferred_element_type=jnp.float32)
    return lagged.reshape(shape[:4] + (table.shape[1],))


def on_device_general(spectra, flags, owners, source_slots):
    shape = spectra.shape
    blocks = spectra.reshape(shape[:4] + (shape[4] // 64, 64))
    power = jnp.mean(blocks * blocks, axis=(2, 3, 5), keepdims=True)
    whitened = (blocks / jnp.sqrt(power + 1e-06)).reshape(shape)
    weighted = whitened * flags.astype(jnp.float32)[:, :, None, None, None]
    table = jnp.asarray(lag_table(shape[4], NLAG, shape[0] * lax.axis_size("win")))
    outputs = []
    for step in range(source_slots.shape[0]):
        chosen = jnp.take(weighted, source_slots[step], axis=1)
        picked = spread(chosen, "sta", owners[step])
        outputs.append(lax.psum(cross(picked, weighted, table), "win"))
    return jnp.stack(outputs)


def solution(mesh):
    small = mesh.shape["sta"] == 16 and mesh.shape["win"] == 2
    return jax.shard_map(
        on_device if small else on_device_general,
        mesh=mesh,
        in_specs=(P("win", "sta", None, None, None), P("win", "sta"), P(), P()),
        out_specs=P(None, None, None, "sta", None, None),
        check_vma=False,
    )
```

```python
import functools
import math

import jax
import jax.numpy as jnp
import numpy as np
from jax import lax
from jax.experimental import pallas as pl
from jax.experimental.pallas import tpu as pltpu
from jax.sharding import PartitionSpec as P

NLAG = 768
LANES = 128
MIB = 1024 * 1024


def lag_table(bins, lags, windows):
    freq = np.arange(bins, dtype=np.int64) + 360
    shift = np.arange(lags, dtype=np.int64) - lags // 2
    phase = np.mod(freq[:, None] * shift[None, :], 7200).astype(np.float32) * np.float32(
        2.0 * math.pi / 7200.0
    )
    scale = np.float32(1.0 / math.sqrt(windows * bins))
    real = (np.cos(phase) * scale).reshape(bins // LANES, 1, LANES, lags)
    imag = (-np.sin(phase) * scale).reshape(bins // LANES, 1, LANES, lags)
    return np.concatenate([real, imag], axis=1).reshape(2 * bins, lags).astype(jnp.bfloat16)


def whiten_kernel(flags_hbm, x_hbm, pieces_ref, rec_ref, flags, x_ref, sems):
    copies = (
        pltpu.make_async_copy(flags_hbm, flags, sems.at[0]),
        pltpu.make_async_copy(x_hbm, x_ref, sems.at[1]),
    )
    for copy in copies:
        copy.start()
    for copy in copies:
        copy.wait()
    wins, stas, comps, _, bins = x_ref.shape
    core = lax.axis_index("win")
    place = ((0, 1 + core), (2 - core, 3))
    tiles = bins // LANES
    lane = lax.broadcasted_iota(jnp.int32, (wins * stas, LANES), 1)
    left = lane < 64
    sums = []
    for w in range(wins):
        for s in range(stas):
            x = x_ref[w, s]
            sums.append(jnp.sum(jnp.sum(x * x, axis=0), axis=0, keepdims=True))
    power = jnp.concatenate(sums, axis=0)
    weight = jnp.concatenate(
        [
            jnp.full((1, LANES), flags[w, s].astype(jnp.float32), jnp.float32)
            for w in range(wins)
            for s in range(stas)
        ],
        axis=0,
    )
    scales = []
    for c in range(tiles):
        tile = power[:, c * LANES : (c + 1) * LANES]
        low = jnp.sum(jnp.where(left, tile, 0.0), axis=1, keepdims=True)
        high = jnp.sum(jnp.where(left, 0.0, tile), axis=1, keepdims=True)
        mean = jnp.where(left, low, high) * (1.0 / (64 * 2 * comps))
        scales.append(weight / jnp.sqrt(mean + 1e-06))
    scale = jnp.concatenate(scales, axis=1)
    for w in range(wins):
        for s in range(stas):
            k = w * stas + s
            weights = scale[k : k + 1]
            for i in range(comps):
                y = x_ref[w, s, i] * weights
                for part in range(2):
                    rec_ref[w, part, pl.ds(i * stas + s, 1), :] = y[part : part + 1]
                    for c in range(tiles):
                        pieces_ref[4 * s + place[w][part], pl.ds(i * tiles + c, 1), :] = y[
                            part : part + 1, c * LANES : (c + 1) * LANES
                        ]
    rest = pieces_ref.shape[1] - comps * tiles
    if rest:
        for k in range(wins * stas * 2):
            pieces_ref[k, pl.ds(comps * tiles, rest), :] = jnp.zeros((rest, LANES), jnp.float32)
    spare = rec_ref.shape[2] - comps * stas
    if spare:
        for w in range(wins):
            for part in range(2):
                rec_ref[w, part, pl.ds(comps * stas, spare), :] = jnp.zeros(
                    (spare, bins), jnp.float32
                )


def whiten(spectra, flags):
    wins, stas, _, comps, bins = spectra.shape
    rows = -(-comps * (bins // LANES) // 8) * 8
    recs = -(-comps * stas // 8) * 8
    return pl.pallas_call(
        whiten_kernel,
        out_shape=(
            jax.ShapeDtypeStruct((wins * stas * 2, rows, LANES), jnp.float32),
            jax.ShapeDtypeStruct((wins, 2, recs, bins), jnp.float32),
        ),
        in_specs=[pl.BlockSpec(memory_space=pltpu.HBM)] * 2,
        out_specs=(
            pl.BlockSpec(memory_space=pltpu.VMEM),
            pl.BlockSpec(memory_space=pltpu.VMEM),
        ),
        scratch_shapes=[
            pltpu.SMEM(flags.shape, jnp.int32),
            pltpu.VMEM((wins, stas, comps, 2, bins), jnp.float32),
            pltpu.SemaphoreType.DMA((2,)),
        ],
        compiler_params=pltpu.CompilerParams(vmem_limit_bytes=61 * MIB),
        name="whiten",
    )(flags, jnp.transpose(spectra, (0, 1, 3, 2, 4)))


def pick_kernel(params, got_ref, before, keep_ref, send_ref):
    half = keep_ref.shape[0]
    for t in range(half):
        keep_ref[t] = got_ref[params[t]]
        send_ref[t] = got_ref[params[half + t]]


def pick(params, got, before, steps):
    shape = jax.ShapeDtypeStruct((steps // 2,) + got.shape[1:], jnp.float32)
    smem = pl.BlockSpec(memory_space=pltpu.SMEM)
    vmem = pl.BlockSpec(memory_space=pltpu.VMEM)
    return pl.pallas_call(
        pick_kernel,
        out_shape=(shape, shape),
        in_specs=[smem, vmem, vmem],
        out_specs=(vmem, vmem),
        compiler_params=pltpu.CompilerParams(vmem_limit_bytes=8 * MIB),
        name="pick",
    )(params, got, before)


def pack_kernel(*refs, count):
    for n, value in enumerate(refs[-1 - count : -1]):
        refs[-1][n] = value[...]


def pack(values, before):
    vmem = pl.BlockSpec(memory_space=pltpu.VMEM)
    return pl.pallas_call(
        functools.partial(pack_kernel, count=len(values)),
        out_shape=jax.ShapeDtypeStruct((len(values),) + values[0].shape, values[0].dtype),
        in_specs=[vmem] * (len(values) + len(before)),
        out_specs=vmem,
        compiler_params=pltpu.CompilerParams(vmem_limit_bytes=8 * MIB),
        cost_estimate=pl.CostEstimate(flops=0, bytes_accessed=20 * MIB, transcendentals=0),
        name="pack",
    )(*before, *values)


def load_kernel(table_hbm, after, out_ref, sem):
    copy = pltpu.make_async_copy(table_hbm, out_ref, sem)
    copy.start()
    copy.wait()


def load(table, after):
    vmem = pl.BlockSpec(memory_space=pltpu.VMEM)
    return pl.pallas_call(
        load_kernel,
        out_shape=jax.ShapeDtypeStruct(table.shape, table.dtype),
        in_specs=[pl.BlockSpec(memory_space=pltpu.HBM), vmem],
        out_specs=vmem,
        scratch_shapes=[pltpu.SemaphoreType.DMA],
        compiler_params=pltpu.CompilerParams(vmem_limit_bytes=8 * MIB),
        cost_estimate=pl.CostEstimate(flops=0, bytes_accessed=5 * MIB, transcendentals=0),
        name="load",
    )(table, after)


def correlate_kernel(params, *refs, count):
    spots_in = [refs[n * count : (n + 1) * count] for n in range(4)]
    receivers_in, table, out_ref, lhs, rec = (
        refs[4 * count : 4 * count + 2],
        *refs[4 * count + 2 :],
    )
    _, groups, steps, _, _ = spots_in[0][0].shape
    offsets = [(k, n) for k in range(count) for n in range(spots_in[0][k].shape[0])]
    depth = len(offsets)
    tiles = receivers_in[0].shape[3] // LANES
    place, core = lax.axis_index("sta") & 3, lax.axis_index("win")
    window, part = (place >> (1 - core)) & 1, (place >> core) & 1
    kinds = ((window, part), (part, window))
    signs = [1.0 - 2.0 * p.astype(jnp.float32) for _, p in kinds]
    for g in range(groups):
        for w in range(2):
            for p in range(2):
                rows = receivers_in[g][kinds[g][0] ^ w, kinds[g][1] ^ p, 0:12, :]
                rec[g, w, p, 0:12, :] = rows
                rec[g, w, p, 12:24, :] = rows
    spots = (((0, 1), (2, 3)), ((0, 2), (1, 3)))
    upper = lax.broadcasted_iota(jnp.int32, (8, LANES), 0) < 4

    def source(spot, g, n, c):
        t, (k, offset), i = n // (3 * depth), offsets[(n // 3) % depth], n % 3
        line = spots_in[spot][k][offset, g, t, pl.ds(i * tiles + c, 1), :]
        return jnp.broadcast_to(line, (8, LANES))

    def chunk(c, carry):
        lanes = pl.ds(pl.multiple_of(c * LANES, LANES), LANES)
        receivers = [
            [[rec[g, w, p, :, lanes] for p in range(2)] for w in range(2)] for g in range(groups)
        ]
        for block in range(steps * depth * 3 // 4):
            real_tiles, imag_tiles = [], []
            for pair in range(2):
                numbers = (block * 4 + pair * 2, block * 4 + pair * 2 + 1)
                real = [0.0] * 3
                imag = [0.0] * 3
                for g in range(groups):
                    part_imag = [0.0] * 3
                    for w in range(2):
                        spread = []
                        for p in range(2):
                            rows = [source(spots[g][w][p], g, n, c) for n in numbers]
                            spread.append((rows[0], jnp.where(upper, rows[0], rows[1]), rows[1]))
                        for k in range(3):
                            ra = receivers[g][w][0][8 * k : 8 * k + 8]
                            rb = receivers[g][w][1][8 * k : 8 * k + 8]
                            a, b = spread[0][k], spread[1][k]
                            real[k] += a * ra + b * rb
                            part_imag[k] += b * ra - a * rb
                    for k in range(3):
                        imag[k] += signs[g] * part_imag[k]
                real_tiles += real
                imag_tiles += imag
            at = pl.ds(block * 48, 48)
            base = c * 2 * LANES
            lhs[at, pl.ds(pl.multiple_of(base, LANES), LANES)] = jnp.concatenate(
                real_tiles, axis=0
            ).astype(jnp.bfloat16)
            lhs[at, pl.ds(pl.multiple_of(base + LANES, LANES), LANES)] = jnp.concatenate(
                imag_tiles, axis=0
            ).astype(jnp.bfloat16)
        return carry

    lax.fori_loop(0, tiles, chunk, 0, unroll=True)
    for n in range(out_ref.shape[3] // 256):
        lags = pl.ds(n * 256, 256)
        result = jnp.dot(lhs[...], table[:, lags], preferred_element_type=jnp.float32)
        for t in range(steps):
            for offset in range(depth):
                first = params[2 * steps + depth * t + offset] * 9
                for k in range(9):
                    row = 4 * ((t * depth + offset) * 9 + k)
                    out_ref[t, first + k, :, lags] = result[row : row + 4]


def correlate(params, sources, own, other, table):
    count = len(sources[0])
    steps = sources[0][0].shape[2]
    depth = sum(value.shape[0] for value in sources[0])
    bins = own.shape[3]
    lags = table.shape[1]
    rows = steps * depth * 3 * 12
    vmem = pl.BlockSpec(memory_space=pltpu.VMEM)
    return pl.pallas_call(
        functools.partial(correlate_kernel, count=count),
        out_shape=jax.ShapeDtypeStruct((steps, depth * 9, 4, lags), jnp.float32),
        in_specs=[pl.BlockSpec(memory_space=pltpu.SMEM)] + [vmem] * (4 * count + 3),
        out_specs=vmem,
        scratch_shapes=[
            pltpu.VMEM((rows, 2 * bins), jnp.bfloat16),
            pltpu.VMEM((2, 2, 2, 24, bins), jnp.float32),
        ],
        compiler_params=pltpu.CompilerParams(vmem_limit_bytes=20 * MIB),
        cost_estimate=pl.CostEstimate(
            flops=4 * rows * bins * lags, bytes_accessed=8 * MIB, transcendentals=0
        ),
        name="correlate",
    )(params, *[value for spot in sources for value in spot], own, other, table)


def write_steps(half, out, core, sems):
    parts = sems.shape[1]
    size = half.shape[1] // parts
    copies = [
        pltpu.make_async_copy(
            half.at[t, pl.ds(n * size, size)],
            out.at[2 * t + core, pl.ds(n * size, size)],
            sems.at[t, n],
        )
        for t in range(half.shape[0])
        for n in range(parts)
    ]
    for copy in copies:
        copy.start()
    for copy in copies:
        copy.wait()


def put_kernel(own, out, sems):
    write_steps(own, out, lax.axis_index("win"), sems)


def put(own):
    return pl.pallas_call(
        put_kernel,
        out_shape=jax.ShapeDtypeStruct((2 * own.shape[0],) + own.shape[1:], own.dtype),
        in_specs=[pl.BlockSpec(memory_space=pltpu.VMEM)],
        out_specs=pl.BlockSpec(memory_space=pltpu.HBM),
        scratch_shapes=[pltpu.SemaphoreType.DMA((own.shape[0], 4))],
        compiler_params=pltpu.CompilerParams(vmem_limit_bytes=8 * MIB),
        name="put",
    )(own)


def join_kernel(other, whole, out, sems, first):
    write_steps(other, out, 2 * first + 1 - lax.axis_index("win"), sems)


def join(other, whole, first):
    hbm = pl.BlockSpec(memory_space=pltpu.HBM)
    return pl.pallas_call(
        functools.partial(join_kernel, first=first),
        out_shape=jax.ShapeDtypeStruct(whole.shape, whole.dtype),
        in_specs=[pl.BlockSpec(memory_space=pltpu.VMEM), hbm],
        out_specs=hbm,
        scratch_shapes=[pltpu.SemaphoreType.DMA((other.shape[0], 4))],
        input_output_aliases={1: 0},
        compiler_params=pltpu.CompilerParams(vmem_limit_bytes=8 * MIB),
        name="join",
    )(other, whole)


def swap(value):
    return lax.ppermute(value, "win", [(0, 1), (1, 0)])


def on_device(spectra, flags, owners, source_slots):
    wins, stas, _, comps, bins = spectra.shape
    steps, sources = source_slots.shape
    at = lax.axis_index("sta")
    core = lax.axis_index("win")
    blocks = lax.axis_size("sta")
    pairs = owners.reshape(steps // 2, 2)
    slots = source_slots.reshape(steps // 2, 2, sources)
    z = at >> 2
    mine = jnp.where(core == 0, slots[:, 0], slots[:, 1])
    held = z ^ jnp.arange(sources, dtype=jnp.int32)
    order = jnp.arange(sources, dtype=jnp.int32)
    found = jnp.sum(
        jnp.where(mine[:, None, :] == held[None, :, None], order[None, None, :], 0), axis=2
    )
    params = jnp.concatenate(
        [
            jnp.where(core == 0, pairs[:, 0], pairs[:, 1]),
            jnp.where(core == 0, pairs[:, 1], pairs[:, 0]),
            found.reshape(-1),
        ]
    ).astype(jnp.int32)
    pieces, own = whiten(spectra, flags)
    other = swap(own)
    got = lax.all_to_all(pieces, "sta", 0, 0)
    keep, send = pick(params, got, other, steps)
    mine = jnp.stack([keep, swap(send)])

    def partner(bits):
        return [(i, i ^ bits) for i in range(blocks)]

    def by_core(first, second):
        bits = (first, second)
        return [(2 * i + c, 2 * (i ^ bits[c]) + c) for i in range(blocks) for c in range(2)]

    def plane(value):
        near = lax.ppermute(value, ("sta", "win"), by_core(1, 2))
        side = lax.ppermute(value, ("sta", "win"), by_core(2, 1))
        return value, near, side, lax.ppermute(value, "sta", partner(3))

    first = plane(mine)
    far, farther = [lax.ppermute(mine, "sta", partner(4 * k)) for k in (2, 3)]
    second = [lax.ppermute(value, "sta", partner(4)) for value in first]
    packed = pack((far, farther), first[1:])
    rest = plane(packed)
    table = load(jnp.asarray(lag_table(bins, NLAG, wins * lax.axis_size("win"))), packed)
    sources_in = [(a[None], b[None], c) for a, b, c in zip(first, second, rest)]
    half = correlate(params, sources_in, own, other, table)
    whole = put(half)
    for step in range(half.shape[0]):
        whole = join(swap(half[step : step + 1]), whole, step)
    return whole.reshape(steps, sources, comps, comps, stas, NLAG).transpose(0, 1, 2, 4, 3, 5)


def spread(value, axis, source):
    kept = jnp.where(lax.axis_index(axis) == source, value, 0).astype(value.dtype)
    return lax.psum(kept, axis)


def cross(picked, receivers, table):
    src_re = picked[:, :, 0][:, :, :, None, None, :]
    src_im = picked[:, :, 1][:, :, :, None, None, :]
    rec_re = receivers[:, :, 0][:, None, None, :, :, :]
    rec_im = receivers[:, :, 1][:, None, None, :, :, :]
    real = jnp.sum(src_re * rec_re + src_im * rec_im, axis=0)
    imag = jnp.sum(src_im * rec_re - src_re * rec_im, axis=0)
    shape = real.shape
    both = jnp.stack(
        [part.reshape(shape[:4] + (shape[4] // LANES, LANES)) for part in (real, imag)], axis=5
    )
    rows = both.reshape(-1, 2 * shape[4]).astype(jnp.bfloat16)
    lagged = jnp.dot(rows, table, preferred_element_type=jnp.float32)
    return lagged.reshape(shape[:4] + (table.shape[1],))


def on_device_general(spectra, flags, owners, source_slots):
    shape = spectra.shape
    blocks = spectra.reshape(shape[:4] + (shape[4] // 64, 64))
    power = jnp.mean(blocks * blocks, axis=(2, 3, 5), keepdims=True)
    whitened = (blocks / jnp.sqrt(power + 1e-06)).reshape(shape)
    weighted = whitened * flags.astype(jnp.float32)[:, :, None, None, None]
    table = jnp.asarray(lag_table(shape[4], NLAG, shape[0] * lax.axis_size("win")))
    outputs = []
    for step in range(source_slots.shape[0]):
        chosen = jnp.take(weighted, source_slots[step], axis=1)
        picked = spread(chosen, "sta", owners[step])
        outputs.append(lax.psum(cross(picked, weighted, table), "win"))
    return jnp.stack(outputs)


def solution(mesh):
    small = mesh.shape["sta"] == 16 and mesh.shape["win"] == 2
    return jax.shard_map(
        on_device if small else on_device_general,
        mesh=mesh,
        in_specs=(P("win", "sta", None, None, None), P("win", "sta"), P(), P()),
        out_specs=P(None, None, None, "sta", None, None),
        check_vma=False,
    )
```

```python
import functools
import math

import jax
import jax.numpy as jnp
import numpy as np
from jax import lax
from jax.experimental import pallas as pl
from jax.experimental.pallas import tpu as pltpu
from jax.sharding import PartitionSpec as P

NLAG = 768
LANES = 128
MIB = 1024 * 1024


def lag_table(bins, lags, windows):
    freq = np.arange(bins, dtype=np.int64) + 360
    shift = np.arange(lags, dtype=np.int64) - lags // 2
    phase = np.mod(freq[:, None] * shift[None, :], 7200).astype(np.float32) * np.float32(
        2.0 * math.pi / 7200.0
    )
    scale = np.float32(1.0 / math.sqrt(windows * bins))
    real = (np.cos(phase) * scale).reshape(bins // LANES, 1, LANES, lags)
    imag = (-np.sin(phase) * scale).reshape(bins // LANES, 1, LANES, lags)
    return np.concatenate([real, imag], axis=1).reshape(2 * bins, lags).astype(jnp.bfloat16)


def whiten_kernel(flags_hbm, x_hbm, pieces_ref, rec_ref, flags, x_ref, sems):
    copies = (
        pltpu.make_async_copy(flags_hbm, flags, sems.at[0]),
        pltpu.make_async_copy(x_hbm, x_ref, sems.at[1]),
    )
    for copy in copies:
        copy.start()
    for copy in copies:
        copy.wait()
    wins, stas, comps, _, bins = x_ref.shape
    core = lax.axis_index("win")
    place = ((0, 1 + core), (2 - core, 3))
    tiles = bins // LANES
    lane = lax.broadcasted_iota(jnp.int32, (wins * stas, LANES), 1)
    left = lane < 64
    sums = []
    for w in range(wins):
        for s in range(stas):
            x = x_ref[w, s]
            sums.append(jnp.sum(jnp.sum(x * x, axis=0), axis=0, keepdims=True))
    power = jnp.concatenate(sums, axis=0)
    weight = jnp.concatenate(
        [
            jnp.full((1, LANES), flags[w, s].astype(jnp.float32), jnp.float32)
            for w in range(wins)
            for s in range(stas)
        ],
        axis=0,
    )
    scales = []
    for c in range(tiles):
        tile = power[:, c * LANES : (c + 1) * LANES]
        low = jnp.sum(jnp.where(left, tile, 0.0), axis=1, keepdims=True)
        high = jnp.sum(jnp.where(left, 0.0, tile), axis=1, keepdims=True)
        mean = jnp.where(left, low, high) * (1.0 / (64 * 2 * comps))
        scales.append(weight / jnp.sqrt(mean + 1e-06))
    scale = jnp.concatenate(scales, axis=1)
    for w in range(wins):
        for s in range(stas):
            k = w * stas + s
            weights = scale[k : k + 1]
            for i in range(comps):
                y = x_ref[w, s, i] * weights
                for part in range(2):
                    rec_ref[w, part, pl.ds(i * stas + s, 1), :] = y[part : part + 1]
                    for c in range(tiles):
                        pieces_ref[4 * s + place[w][part], pl.ds(i * tiles + c, 1), :] = y[
                            part : part + 1, c * LANES : (c + 1) * LANES
                        ]
    rest = pieces_ref.shape[1] - comps * tiles
    if rest:
        for k in range(wins * stas * 2):
            pieces_ref[k, pl.ds(comps * tiles, rest), :] = jnp.zeros((rest, LANES), jnp.float32)
    spare = rec_ref.shape[2] - comps * stas
    if spare:
        for w in range(wins):
            for part in range(2):
                rec_ref[w, part, pl.ds(comps * stas, spare), :] = jnp.zeros(
                    (spare, bins), jnp.float32
                )


def whiten(spectra, flags):
    wins, stas, _, comps, bins = spectra.shape
    rows = -(-comps * (bins // LANES) // 8) * 8
    recs = -(-comps * stas // 8) * 8
    return pl.pallas_call(
        whiten_kernel,
        out_shape=(
            jax.ShapeDtypeStruct((wins * stas * 2, rows, LANES), jnp.float32),
            jax.ShapeDtypeStruct((wins, 2, recs, bins), jnp.float32),
        ),
        in_specs=[pl.BlockSpec(memory_space=pltpu.HBM)] * 2,
        out_specs=(
            pl.BlockSpec(memory_space=pltpu.VMEM),
            pl.BlockSpec(memory_space=pltpu.VMEM),
        ),
        scratch_shapes=[
            pltpu.SMEM(flags.shape, jnp.int32),
            pltpu.VMEM((wins, stas, comps, 2, bins), jnp.float32),
            pltpu.SemaphoreType.DMA((2,)),
        ],
        compiler_params=pltpu.CompilerParams(vmem_limit_bytes=61 * MIB),
        name="whiten",
    )(flags, jnp.transpose(spectra, (0, 1, 3, 2, 4)))


def pick_kernel(params, got_ref, before, keep_ref, send_ref):
    half = keep_ref.shape[0]
    for t in range(half):
        keep_ref[t] = got_ref[params[t]]
        send_ref[t] = got_ref[params[half + t]]


def pick(params, got, before, steps):
    shape = jax.ShapeDtypeStruct((steps // 2,) + got.shape[1:], jnp.float32)
    smem = pl.BlockSpec(memory_space=pltpu.SMEM)
    vmem = pl.BlockSpec(memory_space=pltpu.VMEM)
    return pl.pallas_call(
        pick_kernel,
        out_shape=(shape, shape),
        in_specs=[smem, vmem, vmem],
        out_specs=(vmem, vmem),
        compiler_params=pltpu.CompilerParams(vmem_limit_bytes=8 * MIB),
        name="pick",
    )(params, got, before)


def pack_kernel(*refs, count):
    for n, value in enumerate(refs[-1 - count : -1]):
        refs[-1][n] = value[...]


def pack(values, before):
    vmem = pl.BlockSpec(memory_space=pltpu.VMEM)
    return pl.pallas_call(
        functools.partial(pack_kernel, count=len(values)),
        out_shape=jax.ShapeDtypeStruct((len(values),) + values[0].shape, values[0].dtype),
        in_specs=[vmem] * (len(values) + len(before)),
        out_specs=vmem,
        compiler_params=pltpu.CompilerParams(vmem_limit_bytes=8 * MIB),
        cost_estimate=pl.CostEstimate(flops=0, bytes_accessed=20 * MIB, transcendentals=0),
        name="pack",
    )(*before, *values)


def load_kernel(table_hbm, after, out_ref, sem):
    copy = pltpu.make_async_copy(table_hbm, out_ref, sem)
    copy.start()
    copy.wait()


def load(table, after):
    vmem = pl.BlockSpec(memory_space=pltpu.VMEM)
    return pl.pallas_call(
        load_kernel,
        out_shape=jax.ShapeDtypeStruct(table.shape, table.dtype),
        in_specs=[pl.BlockSpec(memory_space=pltpu.HBM), vmem],
        out_specs=vmem,
        scratch_shapes=[pltpu.SemaphoreType.DMA],
        compiler_params=pltpu.CompilerParams(vmem_limit_bytes=8 * MIB),
        cost_estimate=pl.CostEstimate(flops=0, bytes_accessed=5 * MIB, transcendentals=0),
        name="load",
    )(table, after)


def correlate_kernel(params, *refs, count):
    spots_in = [refs[n * count : (n + 1) * count] for n in range(4)]
    receivers_in, table, out_ref, lhs, rec = (
        refs[4 * count : 4 * count + 2],
        *refs[4 * count + 2 :],
    )
    _, groups, steps, _, _ = spots_in[0][0].shape
    offsets = [(k, n) for k in range(count) for n in range(spots_in[0][k].shape[0])]
    depth = len(offsets)
    tiles = receivers_in[0].shape[3] // LANES
    place, core = lax.axis_index("sta") & 3, lax.axis_index("win")
    window, part = (place >> (1 - core)) & 1, (place >> core) & 1
    kinds = ((window, part), (part, window))
    turn = 1.0 - 2.0 * (window ^ part).astype(jnp.float32)
    sign = 1.0 - 2.0 * part.astype(jnp.float32)
    for g in range(groups):
        for w in range(2):
            for p in range(2):
                rows = receivers_in[g][kinds[g][0] ^ w, kinds[g][1] ^ p, 0:12, :]
                rec[g, w, p, 0:12, :] = rows
                rec[g, w, p, 12:24, :] = rows
    spots = (((0, 1), (2, 3)), ((0, 2), (1, 3)))
    upper = lax.broadcasted_iota(jnp.int32, (8, LANES), 0) < 4

    def source(spot, g, n, c):
        t, (k, offset), i = n // (3 * depth), offsets[(n // 3) % depth], n % 3
        line = spots_in[spot][k][offset, g, t, pl.ds(i * tiles + c, 1), :]
        return jnp.broadcast_to(line, (8, LANES))

    def chunk(c, carry):
        lanes = pl.ds(pl.multiple_of(c * LANES, LANES), LANES)
        receivers = [
            [[rec[g, w, p, :, lanes] for p in range(2)] for w in range(2)] for g in range(groups)
        ]
        for block in range(steps * depth * 3 // 4):
            real_tiles, imag_tiles = [], []
            for pair in range(2):
                numbers = (block * 4 + pair * 2, block * 4 + pair * 2 + 1)
                real = [0.0] * 3
                imag = [0.0] * 3
                for g in range(groups):
                    part_imag = [0.0] * 3
                    for w in range(2):
                        spread = []
                        for p in range(2):
                            rows = [source(spots[g][w][p], g, n, c) for n in numbers]
                            spread.append((rows[0], jnp.where(upper, rows[0], rows[1]), rows[1]))
                        for k in range(3):
                            ra = receivers[g][w][0][8 * k : 8 * k + 8]
                            rb = receivers[g][w][1][8 * k : 8 * k + 8]
                            a, b = spread[0][k], spread[1][k]
                            real[k] += a * ra + b * rb
                            part_imag[k] += b * ra - a * rb
                    for k in range(3):
                        imag[k] += part_imag[k] if g == 0 else turn * part_imag[k]
                real_tiles += real
                imag_tiles += imag
            at = pl.ds(block * 48, 48)
            base = c * 2 * LANES
            lhs[at, pl.ds(pl.multiple_of(base, LANES), LANES)] = jnp.concatenate(
                real_tiles, axis=0
            ).astype(jnp.bfloat16)
            lhs[at, pl.ds(pl.multiple_of(base + LANES, LANES), LANES)] = (
                jnp.concatenate(imag_tiles, axis=0) * sign
            ).astype(jnp.bfloat16)
        return carry

    lax.fori_loop(0, tiles, chunk, 0, unroll=True)
    for n in range(out_ref.shape[3] // 256):
        lags = pl.ds(n * 256, 256)
        result = jnp.dot(lhs[...], table[:, lags], preferred_element_type=jnp.float32)
        for t in range(steps):
            for offset in range(depth):
                first = params[2 * steps + depth * t + offset] * 9
                for k in range(9):
                    row = 4 * ((t * depth + offset) * 9 + k)
                    out_ref[t, first + k, :, lags] = result[row : row + 4]


def correlate(params, sources, own, other, table):
    count = len(sources[0])
    steps = sources[0][0].shape[2]
    depth = sum(value.shape[0] for value in sources[0])
    bins = own.shape[3]
    lags = table.shape[1]
    rows = steps * depth * 3 * 12
    vmem = pl.BlockSpec(memory_space=pltpu.VMEM)
    return pl.pallas_call(
        functools.partial(correlate_kernel, count=count),
        out_shape=jax.ShapeDtypeStruct((steps, depth * 9, 4, lags), jnp.float32),
        in_specs=[pl.BlockSpec(memory_space=pltpu.SMEM)] + [vmem] * (4 * count + 3),
        out_specs=vmem,
        scratch_shapes=[
            pltpu.VMEM((rows, 2 * bins), jnp.bfloat16),
            pltpu.VMEM((2, 2, 2, 24, bins), jnp.float32),
        ],
        compiler_params=pltpu.CompilerParams(vmem_limit_bytes=20 * MIB),
        cost_estimate=pl.CostEstimate(
            flops=4 * rows * bins * lags, bytes_accessed=8 * MIB, transcendentals=0
        ),
        name="correlate",
    )(params, *[value for spot in sources for value in spot], own, other, table)


def write_steps(half, out, core, sems):
    parts = sems.shape[1]
    size = half.shape[1] // parts
    copies = [
        pltpu.make_async_copy(
            half.at[t, pl.ds(n * size, size)],
            out.at[2 * t + core, pl.ds(n * size, size)],
            sems.at[t, n],
        )
        for t in range(half.shape[0])
        for n in range(parts)
    ]
    for copy in copies:
        copy.start()
    for copy in copies:
        copy.wait()


def put_kernel(own, out, sems):
    write_steps(own, out, lax.axis_index("win"), sems)


def put(own):
    return pl.pallas_call(
        put_kernel,
        out_shape=jax.ShapeDtypeStruct((2 * own.shape[0],) + own.shape[1:], own.dtype),
        in_specs=[pl.BlockSpec(memory_space=pltpu.VMEM)],
        out_specs=pl.BlockSpec(memory_space=pltpu.HBM),
        scratch_shapes=[pltpu.SemaphoreType.DMA((own.shape[0], 4))],
        compiler_params=pltpu.CompilerParams(vmem_limit_bytes=8 * MIB),
        name="put",
    )(own)


def join_kernel(other, whole, out, sems, first):
    write_steps(other, out, 2 * first + 1 - lax.axis_index("win"), sems)


def join(other, whole, first):
    hbm = pl.BlockSpec(memory_space=pltpu.HBM)
    return pl.pallas_call(
        functools.partial(join_kernel, first=first),
        out_shape=jax.ShapeDtypeStruct(whole.shape, whole.dtype),
        in_specs=[pl.BlockSpec(memory_space=pltpu.VMEM), hbm],
        out_specs=hbm,
        scratch_shapes=[pltpu.SemaphoreType.DMA((other.shape[0], 4))],
        input_output_aliases={1: 0},
        compiler_params=pltpu.CompilerParams(vmem_limit_bytes=8 * MIB),
        name="join",
    )(other, whole)


def swap(value):
    return lax.ppermute(value, "win", [(0, 1), (1, 0)])


def on_device(spectra, flags, owners, source_slots):
    wins, stas, _, comps, bins = spectra.shape
    steps, sources = source_slots.shape
    at = lax.axis_index("sta")
    core = lax.axis_index("win")
    blocks = lax.axis_size("sta")
    pairs = owners.reshape(steps // 2, 2)
    slots = source_slots.reshape(steps // 2, 2, sources)
    z = at >> 2
    mine = jnp.where(core == 0, slots[:, 0], slots[:, 1])
    held = z ^ jnp.arange(sources, dtype=jnp.int32)
    order = jnp.arange(sources, dtype=jnp.int32)
    found = jnp.sum(
        jnp.where(mine[:, None, :] == held[None, :, None], order[None, None, :], 0), axis=2
    )
    params = jnp.concatenate(
        [
            jnp.where(core == 0, pairs[:, 0], pairs[:, 1]),
            jnp.where(core == 0, pairs[:, 1], pairs[:, 0]),
            found.reshape(-1),
        ]
    ).astype(jnp.int32)
    pieces, own = whiten(spectra, flags)
    other = swap(own)
    got = lax.all_to_all(pieces, "sta", 0, 0)
    keep, send = pick(params, got, other, steps)
    mine = jnp.stack([keep, swap(send)])

    def partner(bits):
        return [(i, i ^ bits) for i in range(blocks)]

    def by_core(first, second):
        bits = (first, second)
        return [(2 * i + c, 2 * (i ^ bits[c]) + c) for i in range(blocks) for c in range(2)]

    def plane(value):
        near = lax.ppermute(value, ("sta", "win"), by_core(1, 2))
        side = lax.ppermute(value, ("sta", "win"), by_core(2, 1))
        return value, near, side, lax.ppermute(value, "sta", partner(3))

    first = plane(mine)
    far, farther = [lax.ppermute(mine, "sta", partner(4 * k)) for k in (2, 3)]
    second = [lax.ppermute(value, "sta", partner(4)) for value in first]
    packed = pack((far, farther), first[1:])
    rest = plane(packed)
    table = load(jnp.asarray(lag_table(bins, NLAG, wins * lax.axis_size("win"))), packed)
    sources_in = [(a[None], b[None], c) for a, b, c in zip(first, second, rest)]
    half = correlate(params, sources_in, own, other, table)
    whole = put(half)
    for step in range(half.shape[0]):
        whole = join(swap(half[step : step + 1]), whole, step)
    return whole.reshape(steps, sources, comps, comps, stas, NLAG).transpose(0, 1, 2, 4, 3, 5)


def spread(value, axis, source):
    kept = jnp.where(lax.axis_index(axis) == source, value, 0).astype(value.dtype)
    return lax.psum(kept, axis)


def cross(picked, receivers, table):
    src_re = picked[:, :, 0][:, :, :, None, None, :]
    src_im = picked[:, :, 1][:, :, :, None, None, :]
    rec_re = receivers[:, :, 0][:, None, None, :, :, :]
    rec_im = receivers[:, :, 1][:, None, None, :, :, :]
    real = jnp.sum(src_re * rec_re + src_im * rec_im, axis=0)
    imag = jnp.sum(src_im * rec_re - src_re * rec_im, axis=0)
    shape = real.shape
    both = jnp.stack(
        [part.reshape(shape[:4] + (shape[4] // LANES, LANES)) for part in (real, imag)], axis=5
    )
    rows = both.reshape(-1, 2 * shape[4]).astype(jnp.bfloat16)
    lagged = jnp.dot(rows, table, preferred_element_type=jnp.float32)
    return lagged.reshape(shape[:4] + (table.shape[1],))


def on_device_general(spectra, flags, owners, source_slots):
    shape = spectra.shape
    blocks = spectra.reshape(shape[:4] + (shape[4] // 64, 64))
    power = jnp.mean(blocks * blocks, axis=(2, 3, 5), keepdims=True)
    whitened = (blocks / jnp.sqrt(power + 1e-06)).reshape(shape)
    weighted = whitened * flags.astype(jnp.float32)[:, :, None, None, None]
    table = jnp.asarray(lag_table(shape[4], NLAG, shape[0] * lax.axis_size("win")))
    outputs = []
    for step in range(source_slots.shape[0]):
        chosen = jnp.take(weighted, source_slots[step], axis=1)
        picked = spread(chosen, "sta", owners[step])
        outputs.append(lax.psum(cross(picked, weighted, table), "win"))
    return jnp.stack(outputs)


def solution(mesh):
    small = mesh.shape["sta"] == 16 and mesh.shape["win"] == 2
    return jax.shard_map(
        on_device if small else on_device_general,
        mesh=mesh,
        in_specs=(P("win", "sta", None, None, None), P("win", "sta"), P(), P()),
        out_specs=P(None, None, None, "sta", None, None),
        check_vma=False,
    )
```
